32 devices in a mesh: mem: 8 (over z, core), lat: 2 (over y), lon: 2 (over x).
Axes of the slice: x: 2, y: 2, z: 4, core: 2. Of those that a mesh axis runs over, the one named last changes fastest.
Arguments:
- controls: float32 [16, 4, 64, 2048], P('mem', None, 'lat', 'lon'), may hold values from -6 to 6
- perturbations: float32 [16, 4, 64, 2048], P('mem', None, 'lat', 'lon'), may hold values from -3 to 3
- obs_mask: int32 [4, 64, 2048], P(None, 'lat', 'lon'), may hold values 0 or 1
- obs_weight: float32 [4, 64, 2048], P(None, 'lat', 'lon'), may hold values from 0.5 to 4
- lat_class: int32 [64], replicated, may hold values from 0 to 15
- lat_table: float32 [16, 15], replicated, may hold values from 0 to 0.25
- lon_table: float32 [16, 15], replicated, may hold values from 0 to 0.25
- lev_table: float32 [4, 15], replicated, may hold values from 0 to 1
Outputs:
- hess_product: float32 [16, 4, 64, 2048], P('mem', None, 'lat', 'lon')
The draws below stay inside these ranges and needn't reach their ends.
All inputs are finite; a program needn't handle non-finite values. No bound on the sum of `obs_mask` on one device may be relied on, other than what follows from the above.
Results may differ from the reference program's by a relative error of at most 0.00005.
Values sent between devices are 32-bit elements; how exact they have to be, the bound alone decides.
A program may use at most 64 MiB of HBM per device.

```python
import math
import jax
import jax.numpy as jnp
from jax import lax

LEV = 4
TAPS = 15
CLASSES = 16
MEMBERS = 16
NLAT = 64
NLON = 2048


def with_ends(drawn, own_key, smallest, top_value):
    spot = [jax.random.randint(jax.random.fold_in(own_key, axis), (), 0, length) for axis, length in enumerate(drawn.shape)]
    widest = drawn.shape.index(max(drawn.shape))
    beside = spot[:widest] + [(spot[widest] + 1) % drawn.shape[widest]] + spot[widest + 1:]
    return drawn.at[tuple(spot)].set(smallest).at[tuple(beside)].set(top_value)


def block_scale(own_key, shape, split, least, high):
    loudness, own = 1.0, jax.random.fold_in(own_key, 6)
    for position, blocks in split:
        draws = jnp.exp(jax.random.uniform(jax.random.fold_in(own, position), (blocks,), jnp.float32, least / len(split), high / len(split)))
        loudness = loudness * jnp.repeat(draws, shape[position] // blocks).reshape([-1 if axis == position else 1 for axis in range(len(shape))])
    return loudness


def gaussian(rng, extent, width, limit, shards=(), held_as=jnp.bfloat16):
    drawn = width * jax.random.normal(rng, extent, jnp.float32)
    if shards:
        drawn = drawn * block_scale(rng, extent, shards, -0.22, 0.18)
    return jnp.clip(drawn, -limit, limit).astype(held_as)


def setup_inputs(seed: int = 0) -> dict:
    arg_keys = jax.random.split(jax.random.key(seed), 9)
    return {
        "controls": gaussian(arg_keys[0], (MEMBERS, LEV, NLAT, NLON), 1.0, 6.0, ((0, 8), (2, 2), (3, 2)), jnp.float32),
        "perturbations": gaussian(arg_keys[1], (MEMBERS, LEV, NLAT, NLON), 0.5, 3.0, ((0, 8), (2, 2), (3, 2)), jnp.float32),
        "obs_mask": with_ends((jax.random.randint(arg_keys[2], (LEV, NLAT, NLON), 0, 2) < 1).astype(jnp.int32), jax.random.fold_in(arg_keys[2], 1), 0, 1),
        "obs_weight": jnp.clip(jnp.exp(math.log(4.0) - 2.0794415 * jax.random.uniform(arg_keys[3], (LEV, NLAT, NLON), jnp.float32) ** block_scale(arg_keys[3], (LEV, NLAT, NLON), ((1, 2), (2, 2)), -0.2, 0.2)), 0.5, 4.0),
        "lat_class": with_ends(jax.random.randint(arg_keys[4], (NLAT,), 0, CLASSES), jax.random.fold_in(arg_keys[4], 1), 0, CLASSES - 1).astype(jnp.int32),
        "lat_table": jnp.clip(jax.random.uniform(arg_keys[5], (CLASSES, TAPS), jnp.float32, 0.0, 0.25), 0.0, 0.25),
        "lon_table": jnp.clip(jax.random.uniform(arg_keys[6], (CLASSES, TAPS), jnp.float32, 0.0, 0.25), 0.0, 0.25),
        "lev_table": jnp.clip(jax.random.uniform(arg_keys[7], (LEV, TAPS), jnp.float32, 0.0, 1.0), 0.0, 1.0),
    }


def lat_forward(padded, coefs):
    row_count = coefs.shape[0]
    total = 0.0
    for tap_index in range(coefs.shape[1]):
        total = total + coefs[:, tap_index][:, None] * padded[:, :, tap_index:tap_index + row_count, :]
    return total


def lat_adjoint(padded, padded_coefs):
    margin = TAPS // 2
    row_count = padded.shape[2] - 2 * margin
    total = 0.0
    for tap_index in range(padded_coefs.shape[1]):
        lower = 2 * margin - tap_index
        total = total + padded_coefs[lower:lower + row_count, tap_index][:, None] * padded[:, :, lower:lower + row_count, :]
    return total


def lon_forward(padded, coefs):
    margin = TAPS // 2
    col_count = padded.shape[3] - 2 * margin
    total = 0.0
    for tap_index in range(coefs.shape[1]):
        total = total + coefs[:, tap_index][:, None] * padded[..., tap_index:tap_index + col_count]
    return total


def lon_adjoint(padded, coefs):
    margin = TAPS // 2
    col_count = padded.shape[3] - 2 * margin
    total = 0.0
    for tap_index in range(coefs.shape[1]):
        lower = 2 * margin - tap_index
        total = total + coefs[:, tap_index][:, None] * padded[..., lower:lower + col_count]
    return total


def lev_forward(field, coefs):
    margin = TAPS // 2
    level_count = field.shape[1]
    padded = jnp.pad(field, ((0, 0), (margin, margin), (0, 0), (0, 0)))
    total = 0.0
    for tap_index in range(coefs.shape[1]):
        total = total + coefs[:, tap_index][:, None, None] * padded[:, tap_index:tap_index + level_count]
    return total


def lev_adjoint(field, coefs):
    margin = TAPS // 2
    level_count = field.shape[1]
    padded = jnp.pad(field, ((0, 0), (margin, margin), (0, 0), (0, 0)))
    padded_coefs = jnp.pad(coefs, ((margin, margin), (0, 0)))
    total = 0.0
    for tap_index in range(coefs.shape[1]):
        lower = 2 * margin - tap_index
        total = total + padded_coefs[lower:lower + level_count, tap_index][:, None, None] * padded[:, lower:lower + level_count]
    return total


def reference(controls, perturbations, obs_mask, obs_weight, lat_class, lat_table, lon_table, lev_table):
    margin = TAPS // 2
    lat_coefs = lat_table[lat_class]
    lon_coefs = lon_table[lat_class]
    lat_padded = jnp.pad(lat_coefs, ((margin, margin), (0, 0)))

    def forward(field):
        padded = jnp.pad(field[None], ((0, 0), (0, 0), (margin, margin), (0, 0)))
        across = lat_forward(padded, lat_coefs)
        padded = jnp.pad(across, ((0, 0), (0, 0), (0, 0), (margin, margin)), mode="wrap")
        return lev_forward(lon_forward(padded, lon_coefs), lev_table)[0]

    def add_member(total, pair):
        return total + pair[1] * forward(pair[0]), None

    increment, unused = lax.scan(add_member, jnp.zeros(controls.shape[1:], jnp.float32), (controls, perturbations))
    weighted = obs_weight * obs_mask.astype(jnp.float32) * increment

    def adjoint(pair):
        backed = lev_adjoint((pair[1] * weighted)[None], lev_table)
        padded = jnp.pad(backed, ((0, 0), (0, 0), (0, 0), (margin, margin)), mode="wrap")
        along = lon_adjoint(padded, lon_coefs)
        padded = jnp.pad(along, ((0, 0), (0, 0), (margin, margin), (0, 0)))
        return pair[0] + lat_adjoint(padded, lat_padded)[0]

    return lax.map(adjoint, (controls, perturbations))
```

```python
import functools

import jax
import jax.numpy as jnp
from jax import lax
from jax.experimental import pallas as pl
from jax.experimental.pallas import tpu as pltpu
from jax.sharding import PartitionSpec as P

LANES = 128
SUB = 8


def by_offset(coefs, offset):
    taps = jnp.arange(coefs.shape[-1], dtype=jnp.int32)
    hit = offset[..., None] == taps
    return jnp.sum(jnp.where(hit, coefs, 0.0), axis=-1)


def lookup(classes, valid, table):
    rows = jnp.arange(table.shape[0], dtype=jnp.int32)
    hit = (classes[:, None] == rows[None, :]) & valid[:, None]
    return jnp.sum(jnp.where(hit[:, :, None], table[None], 0.0), axis=1)


def matrices(lat_class, lat_table, lon_table, lev_table, rows, levels):
    taps = lat_table.shape[1]
    h = taps // 2
    ext = rows + 2 * SUB
    first = lax.axis_index("lat") * rows
    classes = lax.dynamic_slice_in_dim(jnp.pad(lat_class, (SUB, SUB)), first, ext, 0)
    where = first - SUB + jnp.arange(ext, dtype=jnp.int32)
    valid = (where >= 0) & (where < lat_class.shape[0])
    lat_ext = lookup(classes, valid, lat_table)
    lon_ext = lookup(classes, valid, lon_table)
    i = jnp.arange(rows, dtype=jnp.int32)[:, None]
    e = jnp.arange(ext, dtype=jnp.int32)[None, :]
    ahead = by_offset(lat_ext[SUB : SUB + rows][:, None, :], e - SUB - i + h)
    ahead = jnp.where(valid[None, :], ahead, 0.0)
    back = by_offset(lat_ext[None, :, :], i - (e - SUB) + h)
    l = jnp.arange(levels, dtype=jnp.int32)
    mix = by_offset(lev_table[:, None, :], l[None, :] - l[:, None] + h)
    g = mix[:, None, :, None] * ahead[None, :, None, :]
    gt = mix.T[:, None, :, None] * back[None, :, None, :]
    both = jnp.stack([g, gt]).reshape(2, levels * rows, levels * ext)
    return both, lon_ext


def split(x):
    hi = x.astype(jnp.bfloat16)
    return hi, (x - hi.astype(jnp.float32)).astype(jnp.bfloat16)


def kernel(
    dims, ctrl, pert, mask, wgt, g_ref, lonc, out,
    X, Q, Wt, Mk, S, SR, CR, U, Y, D, V, F, R1, R2, WH, B, GS,
    loc, ysend, yrecv, xsend, xrecv, csend, crecv, s1, r1, s2, r2, s3, r3, s4, r4, s5, r5,
):
    n_mem, n_lat, n_lon, members, levels, rows, cols, taps, nt = dims
    h = taps // 2
    nb = cols // LANES + 1
    width = nb * LANES
    rt_n = rows // SUB
    ext = rows + 2 * SUB
    chips = n_mem // 2
    half = nt // 2
    shard = half // chips
    edge = levels * nb
    mem, lat, lon = lax.axis_index("mem"), lax.axis_index("lat"), lax.axis_index("lon")
    z, c = mem // 2, lax.rem(mem, 2)
    sib = mem + 1 - 2 * c
    lon_to = [lax.rem(lon + 1, n_lon)] + ([lax.rem(lon + n_lon - 1, n_lon)] if n_lon > 2 else [])
    lat_to = ((lat - 1, lat > 0, 1), (lat + 1, lat < n_lat - 1, 0))

    main = pl.ds(SUB, rows)
    loads = [
        pltpu.make_async_copy(ctrl, X.at[:, :, main, pl.ds(0, cols)], loc.at[0]),
        pltpu.make_async_copy(pert, Q.at[:, :, main, pl.ds(0, cols)], loc.at[1]),
        pltpu.make_async_copy(wgt, Wt, loc.at[2]),
        pltpu.make_async_copy(mask, Mk, loc.at[3]),
    ]
    for load in loads:
        load.start()

    barrier = pltpu.get_barrier_semaphore()

    def greet(**where):
        pl.semaphore_signal(barrier, inc=1, device_id=where, device_id_type=pl.DeviceIdType.MESH)

    greet(mem=sib)
    for k in range(1, chips):
        greet(mem=lax.rem(z + k, chips) * 2 + c)
    for x in lon_to:
        greet(lon=x)
    for there, exists, _ in lat_to:
        @pl.when(exists)
        def _():
            greet(lat=there)
            for x in lon_to:
                greet(lat=there, lon=x)
    peers = chips + len(lon_to)
    for _, exists, _ in lat_to:
        peers += jnp.where(exists, 1 + len(lon_to), 0)
    pl.semaphore_wait(barrier, peers)

    def remote(src, dst, send, recv, **where):
        return pltpu.make_async_remote_copy(
            src_ref=src, dst_ref=dst, send_sem=send, recv_sem=recv,
            device_id=where, device_id_type=pl.DeviceIdType.MESH,
        )

    def row_copies(side, there):
        mine = pl.ds(0 if side else rows - SUB, SUB)
        its = pl.ds(rows + SUB if side else 0, SUB)
        return [
            remote(src.at[:, :, mine], dst.at[:, :, its, pl.ds(0, cols)], ysend.at[side, a], yrecv.at[side, a], lat=there)
            for a, (src, dst) in enumerate(((ctrl, X), (pert, Q)))
        ]

    for there, exists, side in lat_to:
        @pl.when(exists)
        def _():
            for copy in row_copies(side, there):
                copy.start()

    for t in range(taps):
        B[t] = jnp.broadcast_to(lonc[:, t : t + 1], (ext, LANES))
    n_rows = levels * rows
    for a in range(2):
        hi, lo = split(g_ref[a])
        GS[a, 0:n_rows] = hi
        GS[a, n_rows : 2 * n_rows] = lo

    lane = lax.broadcasted_iota(jnp.int32, (SUB, LANES), 1)
    windows = [(16, 32 * m) for m in range(members)]
    centre = 32 * members - 8
    windows += [(8, centre + 16 * m) for m in range(members)] + [(8, centre + 16 * members)]
    assert centre + 16 * members + 24 <= LANES

    for load in loads:
        load.wait()

    def pack(idx, carry):
        l, r = idx // rt_n, pl.multiple_of(lax.rem(idx, rt_n) * SUB, SUB)
        total = jnp.zeros((SUB, LANES), jnp.float32)
        here, inner = pl.ds(r, SUB), pl.ds(r + SUB, SUB)
        first, last = pl.ds(0, LANES), pl.ds(cols - LANES, LANES)
        wm = [Wt[l, here, at] * Mk[l, here, at].astype(jnp.float32) for at in (first, last)]
        ends = [(X[m, l, inner, first], X[m, l, inner, last]) for m in range(members)]
        ends += [(Q[m, l, inner, first], Q[m, l, inner, last]) for m in range(members)]
        ends += [tuple(wm)]
        for (reach, at), (low, high) in zip(windows, ends):
            part = jnp.where(lane < reach, low, jnp.where(lane >= LANES - reach, high, 0.0))
            total += pltpu.roll(part, at, 1) if at else part
        S[l, here] = total
        return carry

    lax.fori_loop(0, levels * rt_n, pack, 0)

    strips = [remote(S, SR.at[a], xsend.at[a], xrecv.at[a], lon=x) for a, x in enumerate(lon_to)]
    for copy in strips:
        copy.start()

    def corner_copies(side, there):
        mine = pl.ds(0 if side else rows - SUB, SUB)
        return [
            remote(S.at[:, mine], CR.at[side, a], csend.at[side, a], crecv.at[side, a], lat=there, lon=x)
            for a, x in enumerate(lon_to)
        ]

    for there, exists, side in lat_to:
        @pl.when(exists)
        def _():
            for copy in corner_copies(side, there):
                copy.start()

    for side, there, exists in ((0, lat - 1, lat > 0), (1, lat + 1, lat < n_lat - 1)):
        its = pl.ds(rows + SUB if side else 0, SUB)

        @pl.when(jnp.logical_not(exists))
        def _():
            for m in range(members):
                for l in range(levels):
                    X[m, l, its] = jnp.zeros((SUB, width), jnp.float32)
                    Y[m, l, its] = jnp.zeros((SUB, cols), jnp.float32)

    def weigh(idx, carry):
        rt, l = idx // levels, lax.rem(idx, levels)
        r = pl.ds(pl.multiple_of(rt * SUB, SUB), SUB)
        for b in range(nb - 1):
            at = pl.ds(b * LANES, LANES)
            V[idx * nb + b] = Wt[l, r, at] * Mk[l, r, at].astype(jnp.float32)
        return carry

    lax.fori_loop(0, levels * rt_n, weigh, 0)

    def unpack(w, read):
        at = windows[w][1]
        got = read(0) if n_lon == 2 else None
        if got is None:
            a, b = read(1), read(0)
            a = pltpu.roll(a, LANES - at, 1) if at else a
            b = pltpu.roll(b, LANES - at, 1) if at else b
            return jnp.where(lane < LANES // 2, a, b)
        return pltpu.roll(got, LANES - at, 1) if at else got

    for copy in strips:
        copy.wait()
    strip = pl.ds(cols, LANES)

    def spread_strip(idx, carry):
        rt, l = idx // levels, lax.rem(idx, levels)
        r = pl.multiple_of(rt * SUB, SUB)
        for w in range(2 * members + 1):
            value = unpack(w, lambda a: SR[a, l, pl.ds(r, SUB)])
            if w < members:
                X[w, l, pl.ds(r + SUB, SUB), strip] = value
            elif w < 2 * members:
                Q[w - members, l, pl.ds(r + SUB, SUB), strip] = value
            else:
                V[idx * nb + nb - 1] = value
        return carry

    lax.fori_loop(0, levels * rt_n, spread_strip, 0)

    for there, exists, side in lat_to:
        @pl.when(exists)
        def _():
            row_copies(side, there)[0].wait_send()
            for copy in corner_copies(side, there):
                copy.wait_send()
    for side, there, exists in ((0, lat - 1, lat > 0), (1, lat + 1, lat < n_lat - 1)):
        its = pl.ds(rows + SUB if side else 0, SUB)

        @pl.when(exists)
        def _():
            row_copies(side, there)[0].wait_recv()
            for copy in corner_copies(side, there):
                copy.wait_recv()
            for l in range(levels):
                for w in range(2 * members):
                    value = unpack(w, lambda a: CR[side, a, l])
                    if w < members:
                        X[w, l, its, strip] = value
                    else:
                        Q[w - members, l, its, strip] = value

    def product(a, x):
        hi, lo = split(x)
        f32 = jnp.float32
        both = jnp.dot(GS[a], hi, preferred_element_type=f32)
        return both[:n_rows] + both[n_rows:] + jnp.dot(GS[a, 0:n_rows], lo, preferred_element_type=f32)

    for m in range(members):
        for lo_col in range(0, width, 2 * LANES):
            w = min(2 * LANES, width - lo_col)
            x = X[m, :, :, lo_col : lo_col + w].reshape(levels * ext, w)
            U[m, :, :, lo_col : lo_col + w] = product(0, x).reshape(levels, rows, w)

    def along(u, tile, forward):
        total = None
        for t in range(taps):
            s = (h - t) if forward else (t - h)
            moved = pltpu.roll(u, s % width, 1) if s else u
            coef = B[t, pl.ds(pl.multiple_of(tile * SUB, SUB), SUB)]
            term = jnp.concatenate([coef] * nb, axis=1) * moved
            total = term if total is None else total + term
        return total

    def forward(idx, carry):
        rt, l = idx // levels, lax.rem(idx, levels)
        r = pl.multiple_of(rt * SUB, SUB)
        total = None
        for m in range(members):
            term = Q[m, l, pl.ds(r + SUB, SUB)] * along(U[m, l, pl.ds(r, SUB)], rt + 1, True)
            total = term if total is None else total + term
        for b in range(nb):
            D[idx * nb + b] = total[:, b * LANES : (b + 1) * LANES]
        return carry

    lax.fori_loop(0, levels * rt_n, forward, 0)
    for i in range(rt_n * edge, nt):
        D[i] = jnp.zeros((SUB, LANES), jnp.float32)
        V[i] = jnp.zeros((SUB, LANES), jnp.float32)

    base = c * half
    pair = remote(D.at[pl.ds((1 - c) * half, half)], R1, s1, r1, mem=sib)
    pair.start()
    pair.wait_recv()
    to_owner = []
    for k in range(1, chips):
        tz = lax.rem(z + k, chips)
        at = tz * shard

        def add(i, carry, at=at):
            D[base + at + i] += R1[at + i]
            return carry

        lax.fori_loop(0, shard, add, 0)
        copy = remote(D.at[pl.ds(base + at, shard)], R2.at[k - 1], s2.at[k - 1], r2.at[k - 1], mem=tz * 2 + c)
        copy.start()
        to_owner.append(copy)
    for copy in to_owner:
        copy.wait_recv()

    own = z * shard

    def finish(i, carry):
        total = D[base + own + i] + R1[own + i]
        for k in range(1, chips):
            total += R2[k - 1, i]
        F[base + own + i] = total * V[base + own + i]
        return carry

    lax.fori_loop(0, shard, finish, 0)

    mine = F.at[pl.ds(base + own, shard)]
    back = [
        remote(mine, mine, s3.at[k - 1], r3.at[k - 1], mem=lax.rem(z + k, chips) * 2 + c)
        for k in range(1, chips)
    ]
    passed = [remote(mine, mine, s4.at[0], r4.at[0], mem=sib)]
    for copy in back + passed:
        copy.start()
    for k in range(1, chips):
        back[k - 1].wait_recv()
        got = F.at[pl.ds(base + lax.rem(z - k + chips, chips) * shard, shard)]
        copy = remote(got, got, s4.at[k], r4.at[k], mem=sib)
        copy.start()
        passed.append(copy)
    for copy in passed:
        copy.wait_recv()

    def edge_copy(side, there):
        at = 0 if side else (rt_n - 1) * edge
        return remote(F.at[pl.ds(at, edge)], WH.at[side], s5.at[side], r5.at[side], lat=there)

    for there, exists, side in lat_to:
        @pl.when(exists)
        def _():
            edge_copy(side, there).start()

    def backward_tile(l, r, tile, read):
        w = jnp.concatenate([read(b) for b in range(nb)], axis=1)
        for m in range(members):
            Y[m, l, pl.ds(r, SUB)] = along(Q[m, l, pl.ds(r, SUB)] * w, tile, False)[:, :cols]

    def backward(idx, carry):
        rt, l = idx // levels, lax.rem(idx, levels)
        r = pl.multiple_of(rt * SUB + SUB, SUB)
        backward_tile(l, r, rt + 1, lambda b: F[idx * nb + b])
        return carry

    lax.fori_loop(0, levels * rt_n, backward, 0)

    for side, there, exists in ((0, lat - 1, lat > 0), (1, lat + 1, lat < n_lat - 1)):
        tile = rt_n + 1 if side else 0

        @pl.when(exists)
        def _():
            row_copies(side, there)[1].wait_recv()
            edge_copy(side, there).wait_recv()

            def halo(l, carry):
                backward_tile(l, tile * SUB, tile, lambda b: WH[side, l * nb + b])
                return carry

            lax.fori_loop(0, levels, halo, 0)

    for m in range(members):
        for lo_col in range(0, cols, 2 * LANES):
            at = slice(lo_col, lo_col + 2 * LANES)
            y = Y[m, :, :, at].reshape(levels * ext, 2 * LANES)
            out[m, :, :, at] = X[m, :, SUB : SUB + rows, at] + product(1, y).reshape(levels, rows, 2 * LANES)

    pair.wait_send()
    for copy in to_owner + back + passed:
        copy.wait_send()
    for there, exists, side in lat_to:
        @pl.when(exists)
        def _():
            row_copies(side, there)[1].wait_send()
            edge_copy(side, there).wait_send()


def solution(mesh):
    n_mem, n_lat, n_lon = mesh.shape["mem"], mesh.shape["lat"], mesh.shape["lon"]

    def per_device(controls, perturbations, obs_mask, obs_weight, lat_class, lat_table, lon_table, lev_table):
        members, levels, rows, cols = controls.shape
        taps = lat_table.shape[1]
        nb = cols // LANES + 1
        width, ext, rt_n = nb * LANES, rows + 2 * SUB, rows // SUB
        nt = -(-(levels * rt_n * nb) // n_mem) * n_mem
        chips = n_mem // 2
        shard = nt // n_mem
        both, lon_ext = matrices(lat_class, lat_table, lon_table, lev_table, rows, levels)
        dims = (n_mem, n_lat, n_lon, members, levels, rows, cols, taps, nt)
        f32 = jnp.float32
        dma = pltpu.SemaphoreType.DMA
        sides = 1 if n_lon == 2 else 2
        hbm, vmem = pl.BlockSpec(memory_space=pl.ANY), pl.BlockSpec(memory_space=pltpu.VMEM)
        tiles = lambda *n: pltpu.VMEM((*n, SUB, LANES), f32)
        return pl.pallas_call(
            functools.partial(kernel, dims),
            out_shape=jax.ShapeDtypeStruct(controls.shape, f32),
            in_specs=[hbm] * 4 + [vmem] * 2,
            out_specs=vmem,
            scratch_shapes=[
                pltpu.VMEM((members, levels, ext, width), f32),
                pltpu.VMEM((members, levels, ext, width), f32),
                pltpu.VMEM((levels, rows, cols), f32),
                pltpu.VMEM((levels, rows, cols), jnp.int32),
                pltpu.VMEM((levels, rows, LANES), f32),
                pltpu.VMEM((sides, levels, rows, LANES), f32),
                pltpu.VMEM((2, sides, levels, SUB, LANES), f32),
                pltpu.VMEM((members, levels, rows, width), f32),
                pltpu.VMEM((members, levels, ext, cols), f32),
                tiles(nt), tiles(nt), tiles(nt),
                tiles(nt // 2), tiles(max(chips - 1, 1), shard), tiles(2, levels * nb),
                pltpu.VMEM((taps, ext, LANES), f32),
                pltpu.VMEM((2, 2 * levels * rows, levels * ext), jnp.bfloat16),
                dma((4,)), dma((2, 2)), dma((2, 2)), dma((sides,)), dma((sides,)), dma((2, sides)), dma((2, sides)),
                dma(()), dma(()), dma((chips,)), dma((chips,)), dma((chips,)), dma((chips,)),
                dma((chips,)), dma((chips,)), dma((2,)), dma((2,)),
            ],
            compiler_params=pltpu.CompilerParams(
                collective_id=0, has_side_effects=True, vmem_limit_bytes=48 * 1024 * 1024
            ),
        )(controls, perturbations, obs_mask, obs_weight, both, lon_ext)

    return jax.shard_map(
        per_device,
        mesh=mesh,
        in_specs=(
            P("mem", None, "lat", "lon"),
            P("mem", None, "lat", "lon"),
            P(None, "lat", "lon"),
            P(None, "lat", "lon"),
            P(),
            P(),
            P(),
            P(),
        ),
        out_specs=P("mem", None, "lat", "lon"),
        check_vma=False,
    )
```

```python
import functools

import jax
import jax.numpy as jnp
from jax import lax
from jax.experimental import pallas as pl
from jax.experimental.pallas import tpu as pltpu
from jax.sharding import PartitionSpec as P

LANES = 128
SUB = 8


PRECISE = lax.Precision.HIGHEST


def contract(a, b, precision=None):
    return lax.dot_general(
        a, b, (((0,), (0,)), ((), ())), precision=precision, preferred_element_type=jnp.float32
    )


def matrices(lat, classes, lat_tab, lon_tab, lev, G, B, levels, rows):
    n_classes, taps = lat_tab.shape
    n_lat = classes.shape[1]
    h = taps // 2
    ext = rows + 2 * SUB
    wide, n_rows = levels * ext, levels * rows
    start = lat * rows - SUB
    hit = lax.broadcasted_iota(jnp.int32, (n_classes, n_lat), 0) == classes[...]
    block = lax.broadcasted_iota(jnp.int32, (1, wide), 1)
    for l in range(1, levels):
        block = jnp.where(lax.broadcasted_iota(jnp.int32, (1, wide), 1) >= l * ext, block - ext, block)
    level = lax.broadcasted_iota(jnp.int32, (1, wide), 1)
    pick = lax.broadcasted_iota(jnp.int32, (n_lat, wide), 0) == block + start
    one = lambda x: jnp.where(x, 1.0, 0.0)
    onehot = jnp.dot(one(hit), one(pick), preferred_element_type=jnp.float32)
    onehot_ext = onehot[:, :ext]
    lat_rows = contract(onehot_ext, lat_tab[...], PRECISE)
    lat_lanes = contract(lat_tab[...], onehot, PRECISE)
    lon_rows = contract(onehot_ext, lon_tab[...], PRECISE)
    for t in range(taps):
        B[t] = jnp.broadcast_to(lon_rows[:, t : t + 1], (ext, LANES))
    i = lax.broadcasted_iota(jnp.int32, (rows, wide), 0)
    e = block - SUB
    inside = (e + lat * rows >= 0) & (e + lat * rows < n_lat)
    ahead = jnp.zeros((rows, wide), jnp.float32)
    back = jnp.zeros((rows, wide), jnp.float32)
    for t in range(taps):
        ahead = jnp.where((e - i + h == t) & inside, lat_rows[SUB : SUB + rows, t : t + 1], ahead)
        back = jnp.where(i - e + h == t, lat_lanes[t : t + 1, :], back)
    for l in range(levels):
        over, under = jnp.zeros((1, wide), jnp.float32), jnp.zeros((1, wide), jnp.float32)
        for p in range(levels):
            there = (level >= p * ext) & (level < (p + 1) * ext)
            if abs(p - l) <= h:
                over = jnp.where(there, lev[l, p - l + h], over)
                under = jnp.where(there, lev[p, l - p + h], under)
        for a, m in ((0, ahead * over), (1, back * under)):
            hi, lo = split(m)
            G[a, l * rows : (l + 1) * rows] = hi
            G[a, n_rows + l * rows : n_rows + (l + 1) * rows] = lo


def split(x):
    hi = x.astype(jnp.bfloat16)
    return hi, (x - hi.astype(jnp.float32)).astype(jnp.bfloat16)


def kernel(
    dims, ctrl, pert, mask, wgt, classes, lat_tab, lon_tab, lev, out,
    X, Q, Wt, Mk, S, SR, CR, U, Y, D, V, F, R1, R2, WH, B, GS,
    loc, ysend, yrecv, xsend, xrecv, csend, crecv, s1, r1, s2, r2, s3, r3, s4, r4, s5, r5,
):
    n_mem, n_lat, n_lon, members, levels, rows, cols, taps, nt = dims
    h = taps // 2
    nb = cols // LANES + 1
    width = nb * LANES
    rt_n = rows // SUB
    ext = rows + 2 * SUB
    chips = n_mem // 2
    half = nt // 2
    shard = half // chips
    edge = levels * nb
    mem, lat, lon = lax.axis_index("mem"), lax.axis_index("lat"), lax.axis_index("lon")
    z, c = mem // 2, lax.rem(mem, 2)
    sib = mem + 1 - 2 * c
    lon_to = [lax.rem(lon + 1, n_lon)] + ([lax.rem(lon + n_lon - 1, n_lon)] if n_lon > 2 else [])
    lat_to = ((lat - 1, lat > 0, 1), (lat + 1, lat < n_lat - 1, 0))

    main = pl.ds(SUB, rows)
    loads = [
        pltpu.make_async_copy(ctrl, X.at[:, :, main, pl.ds(0, cols)], loc.at[0]),
        pltpu.make_async_copy(pert, Q.at[:, :, main, pl.ds(0, cols)], loc.at[1]),
        pltpu.make_async_copy(wgt, Wt, loc.at[2]),
        pltpu.make_async_copy(mask, Mk, loc.at[3]),
    ]
    for load in loads:
        load.start()

    barrier = pltpu.get_barrier_semaphore()

    def greet(**where):
        pl.semaphore_signal(barrier, inc=1, device_id=where, device_id_type=pl.DeviceIdType.MESH)

    greet(mem=sib)
    for k in range(1, chips):
        greet(mem=lax.rem(z + k, chips) * 2 + c)
    for x in lon_to:
        greet(lon=x)
    for there, exists, _ in lat_to:
        @pl.when(exists)
        def _():
            greet(lat=there)
            for x in lon_to:
                greet(lat=there, lon=x)
    peers = chips + len(lon_to)
    for _, exists, _ in lat_to:
        peers += jnp.where(exists, 1 + len(lon_to), 0)
    pl.semaphore_wait(barrier, peers)

    def remote(src, dst, send, recv, **where):
        return pltpu.make_async_remote_copy(
            src_ref=src, dst_ref=dst, send_sem=send, recv_sem=recv,
            device_id=where, device_id_type=pl.DeviceIdType.MESH,
        )

    def row_copies(side, there):
        mine = pl.ds(0 if side else rows - SUB, SUB)
        its = pl.ds(rows + SUB if side else 0, SUB)
        return [
            remote(src.at[:, :, mine], dst.at[:, :, its, pl.ds(0, cols)], ysend.at[side, a], yrecv.at[side, a], lat=there)
            for a, (src, dst) in enumerate(((ctrl, X), (pert, Q)))
        ]

    for there, exists, side in lat_to:
        @pl.when(exists)
        def _():
            for copy in row_copies(side, there):
                copy.start()

    matrices(lat, classes, lat_tab, lon_tab, lev, GS, B, levels, rows)
    n_rows = levels * rows

    lane = lax.broadcasted_iota(jnp.int32, (SUB, LANES), 1)
    windows = [(16, 32 * m) for m in range(members)]
    centre = 32 * members - 8
    windows += [(8, centre + 16 * m) for m in range(members)] + [(8, centre + 16 * members)]
    assert centre + 16 * members + 24 <= LANES

    for load in loads:
        load.wait()

    def pack(idx, carry):
        l, r = idx // rt_n, pl.multiple_of(lax.rem(idx, rt_n) * SUB, SUB)
        total = jnp.zeros((SUB, LANES), jnp.float32)
        here, inner = pl.ds(r, SUB), pl.ds(r + SUB, SUB)
        first, last = pl.ds(0, LANES), pl.ds(cols - LANES, LANES)
        wm = [Wt[l, here, at] * Mk[l, here, at].astype(jnp.float32) for at in (first, last)]
        ends = [(X[m, l, inner, first], X[m, l, inner, last]) for m in range(members)]
        ends += [(Q[m, l, inner, first], Q[m, l, inner, last]) for m in range(members)]
        ends += [tuple(wm)]
        for (reach, at), (low, high) in zip(windows, ends):
            part = jnp.where(lane < reach, low, jnp.where(lane >= LANES - reach, high, 0.0))
            total += pltpu.roll(part, at, 1) if at else part
        S[l, here] = total
        return carry

    lax.fori_loop(0, levels * rt_n, pack, 0)

    strips = [remote(S, SR.at[a], xsend.at[a], xrecv.at[a], lon=x) for a, x in enumerate(lon_to)]
    for copy in strips:
        copy.start()

    def corner_copies(side, there):
        mine = pl.ds(0 if side else rows - SUB, SUB)
        return [
            remote(S.at[:, mine], CR.at[side, a], csend.at[side, a], crecv.at[side, a], lat=there, lon=x)
            for a, x in enumerate(lon_to)
        ]

    for there, exists, side in lat_to:
        @pl.when(exists)
        def _():
            for copy in corner_copies(side, there):
                copy.start()

    for side, there, exists in ((0, lat - 1, lat > 0), (1, lat + 1, lat < n_lat - 1)):
        its = pl.ds(rows + SUB if side else 0, SUB)

        @pl.when(jnp.logical_not(exists))
        def _():
            for m in range(members):
                for l in range(levels):
                    X[m, l, its] = jnp.zeros((SUB, width), jnp.float32)
                    Y[m, l, its] = jnp.zeros((SUB, cols), jnp.float32)

    def weigh(idx, carry):
        rt, l = idx // levels, lax.rem(idx, levels)
        r = pl.ds(pl.multiple_of(rt * SUB, SUB), SUB)
        for b in range(nb - 1):
            at = pl.ds(b * LANES, LANES)
            V[idx * nb + b] = Wt[l, r, at] * Mk[l, r, at].astype(jnp.float32)
        return carry

    lax.fori_loop(0, levels * rt_n, weigh, 0)

    def unpack(w, read):
        at = windows[w][1]
        got = read(0) if n_lon == 2 else None
        if got is None:
            a, b = read(1), read(0)
            a = pltpu.roll(a, LANES - at, 1) if at else a
            b = pltpu.roll(b, LANES - at, 1) if at else b
            return jnp.where(lane < LANES // 2, a, b)
        return pltpu.roll(got, LANES - at, 1) if at else got

    for copy in strips:
        copy.wait()
    strip = pl.ds(cols, LANES)

    def spread_strip(idx, carry):
        rt, l = idx // levels, lax.rem(idx, levels)
        r = pl.multiple_of(rt * SUB, SUB)
        for w in range(2 * members + 1):
            value = unpack(w, lambda a: SR[a, l, pl.ds(r, SUB)])
            if w < members:
                X[w, l, pl.ds(r + SUB, SUB), strip] = value
            elif w < 2 * members:
                Q[w - members, l, pl.ds(r + SUB, SUB), strip] = value
            else:
                V[idx * nb + nb - 1] = value
        return carry

    lax.fori_loop(0, levels * rt_n, spread_strip, 0)

    for there, exists, side in lat_to:
        @pl.when(exists)
        def _():
            row_copies(side, there)[0].wait_send()
            for copy in corner_copies(side, there):
                copy.wait_send()
    for side, there, exists in ((0, lat - 1, lat > 0), (1, lat + 1, lat < n_lat - 1)):
        its = pl.ds(rows + SUB if side else 0, SUB)

        @pl.when(exists)
        def _():
            row_copies(side, there)[0].wait_recv()
            for copy in corner_copies(side, there):
                copy.wait_recv()
            for l in range(levels):
                for w in range(2 * members):
                    value = unpack(w, lambda a: CR[side, a, l])
                    if w < members:
                        X[w, l, its, strip] = value
                    else:
                        Q[w - members, l, its, strip] = value

    def product(a, x):
        hi, lo = split(x)
        f32 = jnp.float32
        both = jnp.dot(GS[a], hi, preferred_element_type=f32)
        return both[:n_rows] + both[n_rows:] + jnp.dot(GS[a, 0:n_rows], lo, preferred_element_type=f32)

    for m in range(members):
        for lo_col in range(0, width, 2 * LANES):
            w = min(2 * LANES, width - lo_col)
            x = X[m, :, :, lo_col : lo_col + w].reshape(levels * ext, w)
            U[m, :, :, lo_col : lo_col + w] = product(0, x).reshape(levels, rows, w)

    def along(u, tile, forward):
        total = None
        for t in range(taps):
            s = (h - t) if forward else (t - h)
            moved = pltpu.roll(u, s % width, 1) if s else u
            coef = B[t, pl.ds(pl.multiple_of(tile * SUB, SUB), SUB)]
            term = jnp.concatenate([coef] * nb, axis=1) * moved
            total = term if total is None else total + term
        return total

    def forward(idx, carry):
        rt, l = idx // levels, lax.rem(idx, levels)
        r = pl.multiple_of(rt * SUB, SUB)
        total = None
        for m in range(members):
            term = Q[m, l, pl.ds(r + SUB, SUB)] * along(U[m, l, pl.ds(r, SUB)], rt + 1, True)
            total = term if total is None else total + term
        for b in range(nb):
            D[idx * nb + b] = total[:, b * LANES : (b + 1) * LANES]
        return carry

    lax.fori_loop(0, levels * rt_n, forward, 0)
    for i in range(rt_n * edge, nt):
        D[i] = jnp.zeros((SUB, LANES), jnp.float32)
        V[i] = jnp.zeros((SUB, LANES), jnp.float32)

    base = c * half
    pair = remote(D.at[pl.ds((1 - c) * half, half)], R1, s1, r1, mem=sib)
    pair.start()
    pair.wait_recv()
    to_owner = []
    for k in range(1, chips):
        tz = lax.rem(z + k, chips)
        at = tz * shard

        def add(i, carry, at=at):
            D[base + at + i] += R1[at + i]
            return carry

        lax.fori_loop(0, shard, add, 0)
        copy = remote(D.at[pl.ds(base + at, shard)], R2.at[k - 1], s2.at[k - 1], r2.at[k - 1], mem=tz * 2 + c)
        copy.start()
        to_owner.append(copy)
    for copy in to_owner:
        copy.wait_recv()

    own = z * shard

    def finish(i, carry):
        total = D[base + own + i] + R1[own + i]
        for k in range(1, chips):
            total += R2[k - 1, i]
        F[base + own + i] = total * V[base + own + i]
        return carry

    lax.fori_loop(0, shard, finish, 0)

    mine = F.at[pl.ds(base + own, shard)]
    back = [
        remote(mine, mine, s3.at[k - 1], r3.at[k - 1], mem=lax.rem(z + k, chips) * 2 + c)
        for k in range(1, chips)
    ]
    passed = [remote(mine, mine, s4.at[0], r4.at[0], mem=sib)]
    for copy in back + passed:
        copy.start()
    for k in range(1, chips):
        back[k - 1].wait_recv()
        got = F.at[pl.ds(base + lax.rem(z - k + chips, chips) * shard, shard)]
        copy = remote(got, got, s4.at[k], r4.at[k], mem=sib)
        copy.start()
        passed.append(copy)
    for copy in passed:
        copy.wait_recv()

    def edge_copy(side, there):
        at = 0 if side else (rt_n - 1) * edge
        return remote(F.at[pl.ds(at, edge)], WH.at[side], s5.at[side], r5.at[side], lat=there)

    for there, exists, side in lat_to:
        @pl.when(exists)
        def _():
            edge_copy(side, there).start()

    def backward_tile(l, r, tile, read):
        w = jnp.concatenate([read(b) for b in range(nb)], axis=1)
        for m in range(members):
            Y[m, l, pl.ds(r, SUB)] = along(Q[m, l, pl.ds(r, SUB)] * w, tile, False)[:, :cols]

    def backward(idx, carry):
        rt, l = idx // levels, lax.rem(idx, levels)
        r = pl.multiple_of(rt * SUB + SUB, SUB)
        backward_tile(l, r, rt + 1, lambda b: F[idx * nb + b])
        return carry

    lax.fori_loop(0, levels * rt_n, backward, 0)

    for side, there, exists in ((0, lat - 1, lat > 0), (1, lat + 1, lat < n_lat - 1)):
        tile = rt_n + 1 if side else 0

        @pl.when(exists)
        def _():
            row_copies(side, there)[1].wait_recv()
            edge_copy(side, there).wait_recv()

            def halo(l, carry):
                backward_tile(l, tile * SUB, tile, lambda b: WH[side, l * nb + b])
                return carry

            lax.fori_loop(0, levels, halo, 0)

    for m in range(members):
        for lo_col in range(0, cols, 2 * LANES):
            at = slice(lo_col, lo_col + 2 * LANES)
            y = Y[m, :, :, at].reshape(levels * ext, 2 * LANES)
            out[m, :, :, at] = X[m, :, SUB : SUB + rows, at] + product(1, y).reshape(levels, rows, 2 * LANES)

    pair.wait_send()
    for copy in to_owner + back + passed:
        copy.wait_send()
    for there, exists, side in lat_to:
        @pl.when(exists)
        def _():
            row_copies(side, there)[1].wait_send()
            edge_copy(side, there).wait_send()


def solution(mesh):
    n_mem, n_lat, n_lon = mesh.shape["mem"], mesh.shape["lat"], mesh.shape["lon"]

    def per_device(controls, perturbations, obs_mask, obs_weight, lat_class, lat_table, lon_table, lev_table):
        members, levels, rows, cols = controls.shape
        taps = lat_table.shape[1]
        nb = cols // LANES + 1
        width, ext, rt_n = nb * LANES, rows + 2 * SUB, rows // SUB
        nt = -(-(levels * rt_n * nb) // n_mem) * n_mem
        chips = n_mem // 2
        shard = nt // n_mem
        dims = (n_mem, n_lat, n_lon, members, levels, rows, cols, taps, nt)
        f32 = jnp.float32
        dma = pltpu.SemaphoreType.DMA
        sides = 1 if n_lon == 2 else 2
        hbm, vmem = pl.BlockSpec(memory_space=pl.ANY), pl.BlockSpec(memory_space=pltpu.VMEM)
        tiles = lambda *n: pltpu.VMEM((*n, SUB, LANES), f32)
        return pl.pallas_call(
            functools.partial(kernel, dims),
            out_shape=jax.ShapeDtypeStruct(controls.shape, f32),
            in_specs=[hbm] * 4 + [vmem] * 3 + [pl.BlockSpec(memory_space=pltpu.SMEM)],
            out_specs=vmem,
            scratch_shapes=[
                pltpu.VMEM((members, levels, ext, width), f32),
                pltpu.VMEM((members, levels, ext, width), f32),
                pltpu.VMEM((levels, rows, cols), f32),
                pltpu.VMEM((levels, rows, cols), jnp.int32),
                pltpu.VMEM((levels, rows, LANES), f32),
                pltpu.VMEM((sides, levels, rows, LANES), f32),
                pltpu.VMEM((2, sides, levels, SUB, LANES), f32),
                pltpu.VMEM((members, levels, rows, width), f32),
                pltpu.VMEM((members, levels, ext, cols), f32),
                tiles(nt), tiles(nt), tiles(nt),
                tiles(nt // 2), tiles(max(chips - 1, 1), shard), tiles(2, levels * nb),
                pltpu.VMEM((taps, ext, LANES), f32),
                pltpu.VMEM((2, 2 * levels * rows, levels * ext), jnp.bfloat16),
                dma((4,)), dma((2, 2)), dma((2, 2)), dma((sides,)), dma((sides,)), dma((2, sides)), dma((2, sides)),
                dma(()), dma(()), dma((chips,)), dma((chips,)), dma((chips,)), dma((chips,)),
                dma((chips,)), dma((chips,)), dma((2,)), dma((2,)),
            ],
            compiler_params=pltpu.CompilerParams(
                collective_id=0, has_side_effects=True, vmem_limit_bytes=62 * 1024 * 1024
            ),
        )(controls, perturbations, obs_mask, obs_weight, lat_class[None], lat_table, lon_table, lev_table)

    return jax.shard_map(
        per_device,
        mesh=mesh,
        in_specs=(
            P("mem", None, "lat", "lon"),
            P("mem", None, "lat", "lon"),
            P(None, "lat", "lon"),
            P(None, "lat", "lon"),
            P(),
            P(),
            P(),
            P(),
        ),
        out_specs=P("mem", None, "lat", "lon"),
        check_vma=False,
    )
```

```python
import functools

import jax
import jax.numpy as jnp
from jax import lax
from jax.experimental import pallas as pl
from jax.experimental.pallas import tpu as pltpu
from jax.sharding import PartitionSpec as P

LANES = 128
SUB = 8


PRECISE = lax.Precision.HIGHEST


def contract(a, b, precision=None):
    return lax.dot_general(
        a, b, (((0,), (0,)), ((), ())), precision=precision, preferred_element_type=jnp.float32
    )


def matrices(lat, classes, lat_tab, lon_tab, lev, G, B, levels, rows):
    n_classes, taps = lat_tab.shape
    n_lat = classes.shape[1]
    h = taps // 2
    ext = rows + 2 * SUB
    wide, n_rows = levels * ext, levels * rows
    start = lat * rows - SUB
    hit = lax.broadcasted_iota(jnp.int32, (n_classes, n_lat), 0) == classes[...]
    block = lax.broadcasted_iota(jnp.int32, (1, wide), 1)
    for l in range(1, levels):
        block = jnp.where(lax.broadcasted_iota(jnp.int32, (1, wide), 1) >= l * ext, block - ext, block)
    level = lax.broadcasted_iota(jnp.int32, (1, wide), 1)
    pick = lax.broadcasted_iota(jnp.int32, (n_lat, wide), 0) == block + start
    one = lambda x: jnp.where(x, 1.0, 0.0)
    onehot = jnp.dot(one(hit), one(pick), preferred_element_type=jnp.float32)
    onehot_ext = onehot[:, :ext]
    lat_rows = contract(onehot_ext, lat_tab[...], PRECISE)
    lat_lanes = contract(lat_tab[...], onehot, PRECISE)
    lon_rows = contract(onehot_ext, lon_tab[...], PRECISE)
    for t in range(taps):
        B[t] = jnp.broadcast_to(lon_rows[:, t : t + 1], (ext, LANES))
    i = lax.broadcasted_iota(jnp.int32, (rows, wide), 0)
    e = block - SUB
    inside = (e + lat * rows >= 0) & (e + lat * rows < n_lat)
    ahead = jnp.zeros((rows, wide), jnp.float32)
    back = jnp.zeros((rows, wide), jnp.float32)
    for t in range(taps):
        ahead = jnp.where((e - i + h == t) & inside, lat_rows[SUB : SUB + rows, t : t + 1], ahead)
        back = jnp.where(i - e + h == t, lat_lanes[t : t + 1, :], back)
    for l in range(levels):
        over, under = jnp.zeros((1, wide), jnp.float32), jnp.zeros((1, wide), jnp.float32)
        for p in range(levels):
            there = (level >= p * ext) & (level < (p + 1) * ext)
            if abs(p - l) <= h:
                over = jnp.where(there, lev[l, p - l + h], over)
                under = jnp.where(there, lev[p, l - p + h], under)
        for a, m in ((0, ahead * over), (1, back * under)):
            hi, lo = split(m)
            G[a, l * rows : (l + 1) * rows] = hi
            G[a, n_rows + l * rows : n_rows + (l + 1) * rows] = lo


def split(x):
    hi = x.astype(jnp.bfloat16)
    return hi, (x - hi.astype(jnp.float32)).astype(jnp.bfloat16)


def kernel(
    dims, ctrl, pert, mask, wgt, classes, lat_tab, lon_tab, lev, out,
    X, Q, Wt, Mk, S, SR, CR, U, Y, D, V, F, R1, R2, WH, B, GS,
    loc, ysend, yrecv, xsend, xrecv, csend, crecv, s1, r1, s2, r2, s3, r3, s4, r4, s5, r5,
):
    n_mem, n_lat, n_lon, members, levels, rows, cols, taps, nt = dims
    h = taps // 2
    nb = cols // LANES + 1
    width = nb * LANES
    rt_n = rows // SUB
    ext = rows + 2 * SUB
    chips = n_mem // 2
    half = nt // 2
    shard = half // chips
    edge = levels * nb
    n_half = levels * rt_n // 2

    def tile_of(idx):
        return idx // n_half * half + lax.rem(idx, n_half) * nb

    mem, lat, lon = lax.axis_index("mem"), lax.axis_index("lat"), lax.axis_index("lon")
    z, c = mem // 2, lax.rem(mem, 2)
    sib = mem + 1 - 2 * c
    lon_to = [lax.rem(lon + 1, n_lon)] + ([lax.rem(lon + n_lon - 1, n_lon)] if n_lon > 2 else [])
    lat_to = ((lat - 1, lat > 0, 1), (lat + 1, lat < n_lat - 1, 0))

    main = pl.ds(SUB, rows)
    loads = [
        pltpu.make_async_copy(ctrl, X.at[:, :, main, pl.ds(0, cols)], loc.at[0]),
        pltpu.make_async_copy(pert, Q.at[:, :, main, pl.ds(0, cols)], loc.at[1]),
        pltpu.make_async_copy(wgt, Wt, loc.at[2]),
        pltpu.make_async_copy(mask, Mk, loc.at[3]),
    ]
    for load in loads:
        load.start()

    barrier = pltpu.get_barrier_semaphore()

    def greet(**where):
        pl.semaphore_signal(barrier, inc=1, device_id=where, device_id_type=pl.DeviceIdType.MESH)

    greet(mem=sib)
    for k in range(1, chips):
        greet(mem=lax.rem(z + k, chips) * 2 + c)
    for x in lon_to:
        greet(lon=x)
    for there, exists, _ in lat_to:
        @pl.when(exists)
        def _():
            greet(lat=there)
            for x in lon_to:
                greet(lat=there, lon=x)
    peers = chips + len(lon_to)
    for _, exists, _ in lat_to:
        peers += jnp.where(exists, 1 + len(lon_to), 0)
    pl.semaphore_wait(barrier, peers)

    def remote(src, dst, send, recv, **where):
        return pltpu.make_async_remote_copy(
            src_ref=src, dst_ref=dst, send_sem=send, recv_sem=recv,
            device_id=where, device_id_type=pl.DeviceIdType.MESH,
        )

    def row_copies(side, there):
        mine = pl.ds(0 if side else rows - SUB, SUB)
        its = pl.ds(rows + SUB if side else 0, SUB)
        return [
            remote(src.at[:, :, mine], dst.at[:, :, its, pl.ds(0, cols)], ysend.at[side, a], yrecv.at[side, a], lat=there)
            for a, (src, dst) in enumerate(((ctrl, X), (pert, Q)))
        ]

    for there, exists, side in lat_to:
        @pl.when(exists)
        def _():
            row_copies(side, there)[0].start()

    lane = lax.broadcasted_iota(jnp.int32, (SUB, LANES), 1)
    windows = [(16, 32 * m) for m in range(members)]
    centre = 32 * members - 8
    windows += [(8, centre + 16 * m) for m in range(members)] + [(8, centre + 16 * members)]
    assert centre + 16 * members + 24 <= LANES

    for load in loads:
        load.wait()

    def pack(idx, carry):
        l, r = idx // rt_n, pl.multiple_of(lax.rem(idx, rt_n) * SUB, SUB)
        total = jnp.zeros((SUB, LANES), jnp.float32)
        here, inner = pl.ds(r, SUB), pl.ds(r + SUB, SUB)
        first, last = pl.ds(0, LANES), pl.ds(cols - LANES, LANES)
        wm = [Wt[l, here, at] * Mk[l, here, at].astype(jnp.float32) for at in (first, last)]
        ends = [(X[m, l, inner, first], X[m, l, inner, last]) for m in range(members)]
        ends += [(Q[m, l, inner, first], Q[m, l, inner, last]) for m in range(members)]
        ends += [tuple(wm)]
        for (reach, at), (low, high) in zip(windows, ends):
            part = jnp.where(lane < reach, low, jnp.where(lane >= LANES - reach, high, 0.0))
            total += pltpu.roll(part, at, 1) if at else part
        S[l, here] = total
        return carry

    lax.fori_loop(0, levels * rt_n, pack, 0)

    strips = [remote(S, SR.at[a], xsend.at[a], xrecv.at[a], lon=x) for a, x in enumerate(lon_to)]
    for copy in strips:
        copy.start()

    def corner_copies(side, there):
        mine = pl.ds(0 if side else rows - SUB, SUB)
        return [
            remote(S.at[:, mine], CR.at[side, a], csend.at[side, a], crecv.at[side, a], lat=there, lon=x)
            for a, x in enumerate(lon_to)
        ]

    for there, exists, side in lat_to:
        @pl.when(exists)
        def _():
            for copy in corner_copies(side, there):
                copy.start()

    matrices(lat, classes, lat_tab, lon_tab, lev, GS, B, levels, rows)
    n_rows = levels * rows

    for side, there, exists in ((0, lat - 1, lat > 0), (1, lat + 1, lat < n_lat - 1)):
        its = pl.ds(rows + SUB if side else 0, SUB)

        @pl.when(jnp.logical_not(exists))
        def _():
            for m in range(members):
                for l in range(levels):
                    X[m, l, its] = jnp.zeros((SUB, width), jnp.float32)
                    Y[m, l, its] = jnp.zeros((SUB, cols), jnp.float32)

    def weigh(idx, carry):
        rt, l = idx // levels, lax.rem(idx, levels)
        r = pl.ds(pl.multiple_of(rt * SUB, SUB), SUB)
        for b in range(nb - 1):
            at = pl.ds(b * LANES, LANES)
            V[tile_of(idx) + b] = Wt[l, r, at] * Mk[l, r, at].astype(jnp.float32)
        return carry

    lax.fori_loop(0, levels * rt_n, weigh, 0)

    def unpack(w, read):
        at = windows[w][1]
        got = read(0) if n_lon == 2 else None
        if got is None:
            a, b = read(1), read(0)
            a = pltpu.roll(a, LANES - at, 1) if at else a
            b = pltpu.roll(b, LANES - at, 1) if at else b
            return jnp.where(lane < LANES // 2, a, b)
        return pltpu.roll(got, LANES - at, 1) if at else got

    for copy in strips:
        copy.wait()
    strip = pl.ds(cols, LANES)

    def spread_strip(idx, carry):
        rt, l = idx // levels, lax.rem(idx, levels)
        r = pl.multiple_of(rt * SUB, SUB)
        for w in range(2 * members + 1):
            value = unpack(w, lambda a: SR[a, l, pl.ds(r, SUB)])
            if w < members:
                X[w, l, pl.ds(r + SUB, SUB), strip] = value
            elif w < 2 * members:
                Q[w - members, l, pl.ds(r + SUB, SUB), strip] = value
            else:
                V[tile_of(idx) + nb - 1] = value
        return carry

    lax.fori_loop(0, levels * rt_n, spread_strip, 0)

    for there, exists, side in lat_to:
        @pl.when(exists)
        def _():
            row_copies(side, there)[0].wait_send()
            row_copies(side, there)[1].start()
            for copy in corner_copies(side, there):
                copy.wait_send()
    for side, there, exists in ((0, lat - 1, lat > 0), (1, lat + 1, lat < n_lat - 1)):
        its = pl.ds(rows + SUB if side else 0, SUB)

        @pl.when(exists)
        def _():
            row_copies(side, there)[0].wait_recv()
            for copy in corner_copies(side, there):
                copy.wait_recv()
            for l in range(levels):
                for w in range(2 * members):
                    value = unpack(w, lambda a: CR[side, a, l])
                    if w < members:
                        X[w, l, its, strip] = value
                    else:
                        Q[w - members, l, its, strip] = value

    def product(a, x):
        hi, lo = split(x)
        f32 = jnp.float32
        both = jnp.dot(GS[a], hi, preferred_element_type=f32)
        return both[:n_rows] + both[n_rows:] + jnp.dot(GS[a, 0:n_rows], lo, preferred_element_type=f32)

    for m in range(members):
        for lo_col in range(0, width, 2 * LANES):
            w = min(2 * LANES, width - lo_col)
            x = X[m, :, :, lo_col : lo_col + w].reshape(levels * ext, w)
            U[m, :, :, lo_col : lo_col + w] = product(0, x).reshape(levels, rows, w)

    def along(u, tile, forward):
        total = None
        for t in range(taps):
            s = (h - t) if forward else (t - h)
            moved = pltpu.roll(u, s % width, 1) if s else u
            coef = B[t, pl.ds(pl.multiple_of(tile * SUB, SUB), SUB)]
            term = jnp.concatenate([coef] * nb, axis=1) * moved
            total = term if total is None else total + term
        return total

    def forward(idx, carry):
        rt, l = idx // levels, lax.rem(idx, levels)
        r = pl.multiple_of(rt * SUB, SUB)
        total = None
        for m in range(members):
            term = Q[m, l, pl.ds(r + SUB, SUB)] * along(U[m, l, pl.ds(r, SUB)], rt + 1, True)
            total = term if total is None else total + term
        for b in range(nb):
            D[tile_of(idx) + b] = total[:, b * LANES : (b + 1) * LANES]
        return carry

    for g in range(2):
        for i in range(n_half * nb, half):
            D[g * half + i] = jnp.zeros((SUB, LANES), jnp.float32)
            V[g * half + i] = jnp.zeros((SUB, LANES), jnp.float32)

    base = c * half
    other = (1 - c) * n_half
    lax.fori_loop(other, other + n_half, forward, 0)
    pair = remote(D.at[pl.ds((1 - c) * half, half)], R1, s1, r1, mem=sib)
    pair.start()
    lax.fori_loop(c * n_half, c * n_half + n_half, forward, 0)
    pair.wait_recv()
    to_owner = []
    for k in range(1, chips):
        tz = lax.rem(z + k, chips)
        at = tz * shard
        D[pl.ds(base + at, shard)] += R1[pl.ds(at, shard)]
        copy = remote(D.at[pl.ds(base + at, shard)], R2.at[k - 1], s2.at[k - 1], r2.at[k - 1], mem=tz * 2 + c)
        copy.start()
        to_owner.append(copy)
    for copy in to_owner:
        copy.wait_recv()

    own = z * shard

    total = D[pl.ds(base + own, shard)] + R1[pl.ds(own, shard)]
    for k in range(1, chips):
        total += R2[k - 1]
    F[pl.ds(base + own, shard)] = total * V[pl.ds(base + own, shard)]

    mine = F.at[pl.ds(base + own, shard)]
    back = [
        remote(mine, mine, s3.at[k - 1], r3.at[k - 1], mem=lax.rem(z + k, chips) * 2 + c)
        for k in range(1, chips)
    ]
    passed = [remote(mine, mine, s4.at[0], r4.at[0], mem=sib)]
    for copy in back + passed:
        copy.start()
    for k in range(1, chips):
        back[k - 1].wait_recv()
        got = F.at[pl.ds(base + lax.rem(z - k + chips, chips) * shard, shard)]
        copy = remote(got, got, s4.at[k], r4.at[k], mem=sib)
        copy.start()
        passed.append(copy)
    for copy in passed:
        copy.wait_recv()

    def edge_copy(side, there):
        at = 0 if side else half + (rt_n // 2 - 1) * edge
        return remote(F.at[pl.ds(at, edge)], WH.at[side], s5.at[side], r5.at[side], lat=there)

    for there, exists, side in lat_to:
        @pl.when(exists)
        def _():
            edge_copy(side, there).start()

    def backward_tile(l, r, tile, read):
        w = jnp.concatenate([read(b) for b in range(nb)], axis=1)
        for m in range(members):
            Y[m, l, pl.ds(r, SUB)] = along(Q[m, l, pl.ds(r, SUB)] * w, tile, False)[:, :cols]

    def backward(idx, carry):
        rt, l = idx // levels, lax.rem(idx, levels)
        r = pl.multiple_of(rt * SUB + SUB, SUB)
        backward_tile(l, r, rt + 1, lambda b: F[tile_of(idx) + b])
        return carry

    lax.fori_loop(0, levels * rt_n, backward, 0)

    for side, there, exists in ((0, lat - 1, lat > 0), (1, lat + 1, lat < n_lat - 1)):
        tile = rt_n + 1 if side else 0

        @pl.when(exists)
        def _():
            row_copies(side, there)[1].wait_recv()
            edge_copy(side, there).wait_recv()

            def halo(l, carry):
                backward_tile(l, tile * SUB, tile, lambda b: WH[side, l * nb + b])
                return carry

            lax.fori_loop(0, levels, halo, 0)

    for m in range(members):
        for lo_col in range(0, cols, 2 * LANES):
            at = slice(lo_col, lo_col + 2 * LANES)
            y = Y[m, :, :, at].reshape(levels * ext, 2 * LANES)
            out[m, :, :, at] = X[m, :, SUB : SUB + rows, at] + product(1, y).reshape(levels, rows, 2 * LANES)

    pair.wait_send()
    for copy in to_owner + back + passed:
        copy.wait_send()
    for there, exists, side in lat_to:
        @pl.when(exists)
        def _():
            row_copies(side, there)[1].wait_send()
            edge_copy(side, there).wait_send()


def solution(mesh):
    n_mem, n_lat, n_lon = mesh.shape["mem"], mesh.shape["lat"], mesh.shape["lon"]

    def per_device(controls, perturbations, obs_mask, obs_weight, lat_class, lat_table, lon_table, lev_table):
        members, levels, rows, cols = controls.shape
        taps = lat_table.shape[1]
        nb = cols // LANES + 1
        width, ext, rt_n = nb * LANES, rows + 2 * SUB, rows // SUB
        nt = 2 * (-(-(levels * rt_n // 2 * nb) // (n_mem // 2)) * (n_mem // 2))
        chips = n_mem // 2
        shard = nt // n_mem
        dims = (n_mem, n_lat, n_lon, members, levels, rows, cols, taps, nt)
        f32 = jnp.float32
        dma = pltpu.SemaphoreType.DMA
        sides = 1 if n_lon == 2 else 2
        hbm, vmem = pl.BlockSpec(memory_space=pl.ANY), pl.BlockSpec(memory_space=pltpu.VMEM)
        tiles = lambda *n: pltpu.VMEM((*n, SUB, LANES), f32)
        return pl.pallas_call(
            functools.partial(kernel, dims),
            out_shape=jax.ShapeDtypeStruct(controls.shape, f32),
            in_specs=[hbm] * 4 + [vmem] * 3 + [pl.BlockSpec(memory_space=pltpu.SMEM)],
            out_specs=vmem,
            scratch_shapes=[
                pltpu.VMEM((members, levels, ext, width), f32),
                pltpu.VMEM((members, levels, ext, width), f32),
                pltpu.VMEM((levels, rows, cols), f32),
                pltpu.VMEM((levels, rows, cols), jnp.int32),
                pltpu.VMEM((levels, rows, LANES), f32),
                pltpu.VMEM((sides, levels, rows, LANES), f32),
                pltpu.VMEM((2, sides, levels, SUB, LANES), f32),
                pltpu.VMEM((members, levels, rows, width), f32),
                pltpu.VMEM((members, levels, ext, cols), f32),
                tiles(nt), tiles(nt), tiles(nt),
                tiles(nt // 2), tiles(max(chips - 1, 1), shard), tiles(2, levels * nb),
                pltpu.VMEM((taps, ext, LANES), f32),
                pltpu.VMEM((2, 2 * levels * rows, levels * ext), jnp.bfloat16),
                dma((4,)), dma((2, 2)), dma((2, 2)), dma((sides,)), dma((sides,)), dma((2, sides)), dma((2, sides)),
                dma(()), dma(()), dma((chips,)), dma((chips,)), dma((chips,)), dma((chips,)),
                dma((chips,)), dma((chips,)), dma((2,)), dma((2,)),
            ],
            compiler_params=pltpu.CompilerParams(
                collective_id=0, has_side_effects=True, vmem_limit_bytes=62 * 1024 * 1024
            ),
        )(controls, perturbations, obs_mask, obs_weight, lat_class[None], lat_table, lon_table, lev_table)

    return jax.shard_map(
        per_device,
        mesh=mesh,
        in_specs=(
            P("mem", None, "lat", "lon"),
            P("mem", None, "lat", "lon"),
            P(None, "lat", "lon"),
            P(None, "lat", "lon"),
            P(),
            P(),
            P(),
            P(),
        ),
        out_specs=P("mem", None, "lat", "lon"),
        check_vma=False,
    )
```

```python
import functools

import jax
import jax.numpy as jnp
from jax import lax
from jax.experimental import pallas as pl
from jax.experimental.pallas import tpu as pltpu
from jax.sharding import PartitionSpec as P

LANES = 128
SUB = 8


PRECISE = lax.Precision.HIGHEST


def contract(a, b, precision=None):
    return lax.dot_general(
        a, b, (((0,), (0,)), ((), ())), precision=precision, preferred_element_type=jnp.float32
    )


def matrices(lat, classes, lat_tab, lon_tab, lev, G, B, levels, rows):
    n_classes, taps = lat_tab.shape
    n_lat = classes.shape[1]
    h = taps // 2
    ext = rows + 2 * SUB
    wide, n_rows = levels * ext, levels * rows
    start = lat * rows - SUB
    hit = lax.broadcasted_iota(jnp.int32, (n_classes, n_lat), 0) == classes[...]
    block = lax.broadcasted_iota(jnp.int32, (1, wide), 1)
    for l in range(1, levels):
        block = jnp.where(lax.broadcasted_iota(jnp.int32, (1, wide), 1) >= l * ext, block - ext, block)
    level = lax.broadcasted_iota(jnp.int32, (1, wide), 1)
    pick = lax.broadcasted_iota(jnp.int32, (n_lat, wide), 0) == block + start
    one = lambda x: jnp.where(x, 1.0, 0.0)
    onehot = jnp.dot(one(hit), one(pick), preferred_element_type=jnp.float32)
    onehot_ext = onehot[:, :ext]
    lat_rows = contract(onehot_ext, lat_tab[...], PRECISE)
    lat_lanes = contract(lat_tab[...], onehot, PRECISE)
    lon_rows = contract(onehot_ext, lon_tab[...], PRECISE)
    for t in range(taps):
        B[t] = jnp.broadcast_to(lon_rows[:, t : t + 1], (ext, LANES))
    i = lax.broadcasted_iota(jnp.int32, (rows, wide), 0)
    e = block - SUB
    inside = (e + lat * rows >= 0) & (e + lat * rows < n_lat)
    ahead = jnp.zeros((rows, wide), jnp.float32)
    back = jnp.zeros((rows, wide), jnp.float32)
    for t in range(taps):
        ahead = jnp.where((e - i + h == t) & inside, lat_rows[SUB : SUB + rows, t : t + 1], ahead)
        back = jnp.where(i - e + h == t, lat_lanes[t : t + 1, :], back)
    for l in range(levels):
        over, under = jnp.zeros((1, wide), jnp.float32), jnp.zeros((1, wide), jnp.float32)
        for p in range(levels):
            there = (level >= p * ext) & (level < (p + 1) * ext)
            if abs(p - l) <= h:
                over = jnp.where(there, lev[l, p - l + h], over)
                under = jnp.where(there, lev[p, l - p + h], under)
        for a, m in ((0, ahead * over), (1, back * under)):
            hi, lo = split(m)
            G[a, l * rows : (l + 1) * rows] = hi
            G[a, n_rows + l * rows : n_rows + (l + 1) * rows] = lo


def split(x):
    hi = x.astype(jnp.bfloat16)
    return hi, (x - hi.astype(jnp.float32)).astype(jnp.bfloat16)


def kernel(
    dims, ctrl, pert, mask, wgt, classes, lat_tab, lon_tab, lev, out,
    X, Q, Wt, Mk, S, SR, CR, U, Y, D, V, F, R1, R2, WH, B, GS,
    loc, ysend, yrecv, xsend, xrecv, csend, crecv, s1, r1, s2, r2, s3, r3, s4, r4, s5, r5,
):
    n_mem, n_lat, n_lon, members, levels, rows, cols, taps, nt = dims
    h = taps // 2
    nb = cols // LANES + 1
    width = nb * LANES
    rt_n = rows // SUB
    ext = rows + 2 * SUB
    chips = n_mem // 2
    half = nt // 2
    shard = half // chips
    edge = levels * nb
    n_half = levels * rt_n // 2

    def tile_of(idx):
        return idx // n_half * half + lax.rem(idx, n_half) * nb

    mem, lat, lon = lax.axis_index("mem"), lax.axis_index("lat"), lax.axis_index("lon")
    z, c = mem // 2, lax.rem(mem, 2)
    sib = mem + 1 - 2 * c
    lon_to = [lax.rem(lon + 1, n_lon)] + ([lax.rem(lon + n_lon - 1, n_lon)] if n_lon > 2 else [])
    lat_to = ((lat - 1, lat > 0, 1), (lat + 1, lat < n_lat - 1, 0))

    main = pl.ds(SUB, rows)
    loads = [
        pltpu.make_async_copy(ctrl, X.at[:, :, main, pl.ds(0, cols)], loc.at[0]),
        pltpu.make_async_copy(pert, Q.at[:, :, main, pl.ds(0, cols)], loc.at[1]),
        pltpu.make_async_copy(wgt, Wt, loc.at[2]),
        pltpu.make_async_copy(mask, Mk, loc.at[3]),
    ]
    for load in loads:
        load.start()

    barrier = pltpu.get_barrier_semaphore()

    def greet(**where):
        pl.semaphore_signal(barrier, inc=1, device_id=where, device_id_type=pl.DeviceIdType.MESH)

    greet(mem=sib)
    for k in range(1, chips):
        greet(mem=lax.rem(z + k, chips) * 2 + c)
    for x in lon_to:
        greet(lon=x)
    for there, exists, _ in lat_to:
        @pl.when(exists)
        def _():
            greet(lat=there)
            greet(lat=there, mem=sib)
            for x in lon_to:
                greet(lat=there, lon=x)
    peers = chips + len(lon_to)
    for _, exists, _ in lat_to:
        peers += jnp.where(exists, 2 + len(lon_to), 0)
    pl.semaphore_wait(barrier, peers)

    def remote(src, dst, send, recv, **where):
        return pltpu.make_async_remote_copy(
            src_ref=src, dst_ref=dst, send_sem=send, recv_sem=recv,
            device_id=where, device_id_type=pl.DeviceIdType.MESH,
        )

    def row_copies(side, there):
        mine = pl.ds(0 if side else rows - SUB, SUB)
        its = pl.ds(rows + SUB if side else 0, SUB)
        return [
            remote(src.at[:, :, mine], dst.at[:, :, its, pl.ds(0, cols)], ysend.at[side, a], yrecv.at[side, a], lat=there)
            for a, (src, dst) in enumerate(((ctrl, X), (pert, Q)))
        ]

    for there, exists, side in lat_to:
        @pl.when(exists)
        def _():
            row_copies(side, there)[0].start()

    lane = lax.broadcasted_iota(jnp.int32, (SUB, LANES), 1)
    windows = [(16, 32 * m) for m in range(members)]
    centre = 32 * members - 8
    windows += [(8, centre + 16 * m) for m in range(members)] + [(8, centre + 16 * members)]
    assert centre + 16 * members + 24 <= LANES

    for load in loads:
        load.wait()

    def pack(idx, carry):
        l, r = idx // rt_n, pl.multiple_of(lax.rem(idx, rt_n) * SUB, SUB)
        total = jnp.zeros((SUB, LANES), jnp.float32)
        here, inner = pl.ds(r, SUB), pl.ds(r + SUB, SUB)
        first, last = pl.ds(0, LANES), pl.ds(cols - LANES, LANES)
        wm = [Wt[l, here, at] * Mk[l, here, at].astype(jnp.float32) for at in (first, last)]
        ends = [(X[m, l, inner, first], X[m, l, inner, last]) for m in range(members)]
        ends += [(Q[m, l, inner, first], Q[m, l, inner, last]) for m in range(members)]
        ends += [tuple(wm)]
        for (reach, at), (low, high) in zip(windows, ends):
            part = jnp.where(lane < reach, low, jnp.where(lane >= LANES - reach, high, 0.0))
            total += pltpu.roll(part, at, 1) if at else part
        S[l, here] = total
        return carry

    lax.fori_loop(0, levels * rt_n, pack, 0)

    strips = [remote(S, SR.at[a], xsend.at[a], xrecv.at[a], lon=x) for a, x in enumerate(lon_to)]
    for copy in strips:
        copy.start()

    def corner_copies(side, there):
        mine = pl.ds(0 if side else rows - SUB, SUB)
        return [
            remote(S.at[:, mine], CR.at[side, a], csend.at[side, a], crecv.at[side, a], lat=there, lon=x)
            for a, x in enumerate(lon_to)
        ]

    for there, exists, side in lat_to:
        @pl.when(exists)
        def _():
            for copy in corner_copies(side, there):
                copy.start()

    matrices(lat, classes, lat_tab, lon_tab, lev, GS, B, levels, rows)
    n_rows = levels * rows

    for side, there, exists in ((0, lat - 1, lat > 0), (1, lat + 1, lat < n_lat - 1)):
        its = pl.ds(rows + SUB if side else 0, SUB)

        @pl.when(jnp.logical_not(exists))
        def _():
            for m in range(members):
                for l in range(levels):
                    X[m, l, its] = jnp.zeros((SUB, width), jnp.float32)
                    Y[m, l, its] = jnp.zeros((SUB, cols), jnp.float32)

    def weigh(idx, carry):
        rt, l = idx // levels, lax.rem(idx, levels)
        r = pl.ds(pl.multiple_of(rt * SUB, SUB), SUB)
        for b in range(nb - 1):
            at = pl.ds(b * LANES, LANES)
            V[tile_of(idx) + b] = Wt[l, r, at] * Mk[l, r, at].astype(jnp.float32)
        return carry

    lax.fori_loop(0, levels * rt_n, weigh, 0)

    def unpack(w, read):
        at = windows[w][1]
        got = read(0) if n_lon == 2 else None
        if got is None:
            a, b = read(1), read(0)
            a = pltpu.roll(a, LANES - at, 1) if at else a
            b = pltpu.roll(b, LANES - at, 1) if at else b
            return jnp.where(lane < LANES // 2, a, b)
        return pltpu.roll(got, LANES - at, 1) if at else got

    for copy in strips:
        copy.wait()
    strip = pl.ds(cols, LANES)

    def spread_strip(idx, carry):
        rt, l = idx // levels, lax.rem(idx, levels)
        r = pl.multiple_of(rt * SUB, SUB)
        for w in range(2 * members + 1):
            value = unpack(w, lambda a: SR[a, l, pl.ds(r, SUB)])
            if w < members:
                X[w, l, pl.ds(r + SUB, SUB), strip] = value
            elif w < 2 * members:
                Q[w - members, l, pl.ds(r + SUB, SUB), strip] = value
            else:
                V[tile_of(idx) + nb - 1] = value
        return carry

    lax.fori_loop(0, levels * rt_n, spread_strip, 0)

    for there, exists, side in lat_to:
        @pl.when(exists)
        def _():
            row_copies(side, there)[0].wait_send()
            row_copies(side, there)[1].start()
            for copy in corner_copies(side, there):
                copy.wait_send()
    for side, there, exists in ((0, lat - 1, lat > 0), (1, lat + 1, lat < n_lat - 1)):
        its = pl.ds(rows + SUB if side else 0, SUB)

        @pl.when(exists)
        def _():
            row_copies(side, there)[0].wait_recv()
            for copy in corner_copies(side, there):
                copy.wait_recv()
            for l in range(levels):
                for w in range(2 * members):
                    value = unpack(w, lambda a: CR[side, a, l])
                    if w < members:
                        X[w, l, its, strip] = value
                    else:
                        Q[w - members, l, its, strip] = value

    def product(a, x):
        hi, lo = split(x)
        f32 = jnp.float32
        both = jnp.dot(GS[a], hi, preferred_element_type=f32)
        return both[:n_rows] + both[n_rows:] + jnp.dot(GS[a, 0:n_rows], lo, preferred_element_type=f32)

    for m in range(members):
        for lo_col in range(0, width, 2 * LANES):
            w = min(2 * LANES, width - lo_col)
            x = X[m, :, :, lo_col : lo_col + w].reshape(levels * ext, w)
            U[m, :, :, lo_col : lo_col + w] = product(0, x).reshape(levels, rows, w)

    def along(u, tile, forward):
        total = None
        for t in range(taps):
            s = (h - t) if forward else (t - h)
            moved = pltpu.roll(u, s % width, 1) if s else u
            coef = B[t, pl.ds(pl.multiple_of(tile * SUB, SUB), SUB)]
            term = jnp.concatenate([coef] * nb, axis=1) * moved
            total = term if total is None else total + term
        return total

    def forward(idx, carry):
        rt, l = idx // levels, lax.rem(idx, levels)
        r = pl.multiple_of(rt * SUB, SUB)
        total = None
        for m in range(members):
            term = Q[m, l, pl.ds(r + SUB, SUB)] * along(U[m, l, pl.ds(r, SUB)], rt + 1, True)
            total = term if total is None else total + term
        for b in range(nb):
            D[tile_of(idx) + b] = total[:, b * LANES : (b + 1) * LANES]
        return carry

    for g in range(2):
        for i in range(n_half * nb, half):
            D[g * half + i] = jnp.zeros((SUB, LANES), jnp.float32)
            V[g * half + i] = jnp.zeros((SUB, LANES), jnp.float32)

    base = c * half
    other = (1 - c) * n_half
    lax.fori_loop(other, other + n_half, forward, 0)
    pair = remote(D.at[pl.ds((1 - c) * half, half)], R1, s1, r1, mem=sib)
    pair.start()
    lax.fori_loop(c * n_half, c * n_half + n_half, forward, 0)
    pair.wait_recv()
    to_owner = []
    for k in range(1, chips):
        tz = lax.rem(z + k, chips)
        at = tz * shard
        D[pl.ds(base + at, shard)] += R1[pl.ds(at, shard)]
        copy = remote(D.at[pl.ds(base + at, shard)], R2.at[k - 1], s2.at[k - 1], r2.at[k - 1], mem=tz * 2 + c)
        copy.start()
        to_owner.append(copy)
    for copy in to_owner:
        copy.wait_recv()

    own = z * shard

    total = D[pl.ds(base + own, shard)] + R1[pl.ds(own, shard)]
    for k in range(1, chips):
        total += R2[k - 1]
    F[pl.ds(base + own, shard)] = total * V[pl.ds(base + own, shard)]

    mine = F.at[pl.ds(base + own, shard)]
    back = [
        remote(mine, mine, s3.at[k - 1], r3.at[k - 1], mem=lax.rem(z + k, chips) * 2 + c)
        for k in range(1, chips)
    ]
    passed = [remote(mine, mine, s4.at[0], r4.at[0], mem=sib)]
    for copy in back + passed:
        copy.start()
    for k in range(1, chips):
        back[k - 1].wait_recv()
        got = F.at[pl.ds(base + lax.rem(z - k + chips, chips) * shard, shard)]
        copy = remote(got, got, s4.at[k], r4.at[k], mem=sib)
        copy.start()
        passed.append(copy)

    def edge_copies(side, there):
        at = 0 if side else half + (rt_n // 2 - 1) * edge
        return [
            remote(F.at[pl.ds(at, edge)], WH.at[side], s5.at[side, a], r5.at[side], lat=there, mem=m)
            for a, m in enumerate((mem, sib))
        ]

    for there, exists, side in lat_to:
        @pl.when(exists & (c == 1 - side))
        def _():
            for copy in edge_copies(side, there):
                copy.start()

    def backward_tile(l, r, tile, read):
        w = jnp.concatenate([read(b) for b in range(nb)], axis=1)
        for m in range(members):
            Y[m, l, pl.ds(r, SUB)] = along(Q[m, l, pl.ds(r, SUB)] * w, tile, False)[:, :cols]

    def backward(idx, carry):
        rt, l = idx // levels, lax.rem(idx, levels)
        r = pl.multiple_of(rt * SUB + SUB, SUB)
        backward_tile(l, r, rt + 1, lambda b: F[tile_of(idx) + b])
        return carry

    lax.fori_loop(c * n_half, c * n_half + n_half, backward, 0)
    for copy in passed:
        copy.wait_recv()
    lax.fori_loop(other, other + n_half, backward, 0)

    for side, there, exists in ((0, lat - 1, lat > 0), (1, lat + 1, lat < n_lat - 1)):
        tile = rt_n + 1 if side else 0

        @pl.when(exists)
        def _():
            row_copies(side, there)[1].wait_recv()
            edge_copies(side, there)[0].wait_recv()

            def halo(l, carry):
                backward_tile(l, tile * SUB, tile, lambda b: WH[side, l * nb + b])
                return carry

            lax.fori_loop(0, levels, halo, 0)

    for m in range(members):
        for lo_col in range(0, cols, 2 * LANES):
            at = slice(lo_col, lo_col + 2 * LANES)
            y = Y[m, :, :, at].reshape(levels * ext, 2 * LANES)
            out[m, :, :, at] = X[m, :, SUB : SUB + rows, at] + product(1, y).reshape(levels, rows, 2 * LANES)

    pair.wait_send()
    for copy in to_owner + back + passed:
        copy.wait_send()
    for there, exists, side in lat_to:
        @pl.when(exists)
        def _():
            row_copies(side, there)[1].wait_send()

        @pl.when(exists & (c == 1 - side))
        def _():
            for copy in edge_copies(side, there):
                copy.wait_send()


def solution(mesh):
    n_mem, n_lat, n_lon = mesh.shape["mem"], mesh.shape["lat"], mesh.shape["lon"]

    def per_device(controls, perturbations, obs_mask, obs_weight, lat_class, lat_table, lon_table, lev_table):
        members, levels, rows, cols = controls.shape
        taps = lat_table.shape[1]
        nb = cols // LANES + 1
        width, ext, rt_n = nb * LANES, rows + 2 * SUB, rows // SUB
        nt = 2 * (-(-(levels * rt_n // 2 * nb) // (n_mem // 2)) * (n_mem // 2))
        chips = n_mem // 2
        shard = nt // n_mem
        dims = (n_mem, n_lat, n_lon, members, levels, rows, cols, taps, nt)
        f32 = jnp.float32
        dma = pltpu.SemaphoreType.DMA
        sides = 1 if n_lon == 2 else 2
        hbm, vmem = pl.BlockSpec(memory_space=pl.ANY), pl.BlockSpec(memory_space=pltpu.VMEM)
        tiles = lambda *n: pltpu.VMEM((*n, SUB, LANES), f32)
        return pl.pallas_call(
            functools.partial(kernel, dims),
            out_shape=jax.ShapeDtypeStruct(controls.shape, f32),
            in_specs=[hbm] * 4 + [vmem] * 3 + [pl.BlockSpec(memory_space=pltpu.SMEM)],
            out_specs=vmem,
            scratch_shapes=[
                pltpu.VMEM((members, levels, ext, width), f32),
                pltpu.VMEM((members, levels, ext, width), f32),
                pltpu.VMEM((levels, rows, cols), f32),
                pltpu.VMEM((levels, rows, cols), jnp.int32),
                pltpu.VMEM((levels, rows, LANES), f32),
                pltpu.VMEM((sides, levels, rows, LANES), f32),
                pltpu.VMEM((2, sides, levels, SUB, LANES), f32),
                pltpu.VMEM((members, levels, rows, width), f32),
                pltpu.VMEM((members, levels, ext, cols), f32),
                tiles(nt), tiles(nt), tiles(nt),
                tiles(nt // 2), tiles(max(chips - 1, 1), shard), tiles(2, levels * nb),
                pltpu.VMEM((taps, ext, LANES), f32),
                pltpu.VMEM((2, 2 * levels * rows, levels * ext), jnp.bfloat16),
                dma((4,)), dma((2, 2)), dma((2, 2)), dma((sides,)), dma((sides,)), dma((2, sides)), dma((2, sides)),
                dma(()), dma(()), dma((chips,)), dma((chips,)), dma((chips,)), dma((chips,)),
                dma((chips,)), dma((chips,)), dma((2, 2)), dma((2,)),
            ],
            compiler_params=pltpu.CompilerParams(
                collective_id=0, has_side_effects=True, vmem_limit_bytes=62 * 1024 * 1024
            ),
        )(controls, perturbations, obs_mask, obs_weight, lat_class[None], lat_table, lon_table, lev_table)

    return jax.shard_map(
        per_device,
        mesh=mesh,
        in_specs=(
            P("mem", None, "lat", "lon"),
            P("mem", None, "lat", "lon"),
            P(None, "lat", "lon"),
            P(None, "lat", "lon"),
            P(),
            P(),
            P(),
            P(),
        ),
        out_specs=P("mem", None, "lat", "lon"),
        check_vma=False,
    )
```

```python
import functools

import jax
import jax.numpy as jnp
from jax import lax
from jax.experimental import pallas as pl
from jax.experimental.pallas import tpu as pltpu
from jax.sharding import PartitionSpec as P

LANES = 128
SUB = 8


PRECISE = lax.Precision.HIGHEST


def contract(a, b, precision=None):
    return lax.dot_general(
        a, b, (((0,), (0,)), ((), ())), precision=precision, preferred_element_type=jnp.float32
    )


def matrices(lat, classes, lat_tab, lon_tab, lev, G, B, levels, rows):
    n_classes, taps = lat_tab.shape
    n_lat = classes.shape[1]
    h = taps // 2
    ext = rows + 2 * SUB
    wide, n_rows = levels * ext, levels * rows
    start = lat * rows - SUB
    hit = lax.broadcasted_iota(jnp.int32, (n_classes, n_lat), 0) == classes[...]
    block = lax.broadcasted_iota(jnp.int32, (1, wide), 1)
    for l in range(1, levels):
        block = jnp.where(lax.broadcasted_iota(jnp.int32, (1, wide), 1) >= l * ext, block - ext, block)
    level = lax.broadcasted_iota(jnp.int32, (1, wide), 1)
    pick = lax.broadcasted_iota(jnp.int32, (n_lat, wide), 0) == block + start
    one = lambda x: jnp.where(x, 1.0, 0.0)
    onehot = jnp.dot(one(hit), one(pick), preferred_element_type=jnp.float32)
    onehot_ext = onehot[:, :ext]
    lat_rows = contract(onehot_ext, lat_tab[...], PRECISE)
    lat_lanes = contract(lat_tab[...], onehot, PRECISE)
    lon_rows = contract(onehot_ext, lon_tab[...], PRECISE)
    for t in range(taps):
        B[t] = jnp.broadcast_to(lon_rows[:, t : t + 1], (ext, LANES))
    i = lax.broadcasted_iota(jnp.int32, (rows, wide), 0)
    e = block - SUB
    inside = (e + lat * rows >= 0) & (e + lat * rows < n_lat)
    ahead = jnp.zeros((rows, wide), jnp.float32)
    back = jnp.zeros((rows, wide), jnp.float32)
    for t in range(taps):
        ahead = jnp.where((e - i + h == t) & inside, lat_rows[SUB : SUB + rows, t : t + 1], ahead)
        back = jnp.where(i - e + h == t, lat_lanes[t : t + 1, :], back)
    for l in range(levels):
        over, under = jnp.zeros((1, wide), jnp.float32), jnp.zeros((1, wide), jnp.float32)
        for p in range(levels):
            there = (level >= p * ext) & (level < (p + 1) * ext)
            if abs(p - l) <= h:
                over = jnp.where(there, lev[l, p - l + h], over)
                under = jnp.where(there, lev[p, l - p + h], under)
        for a, m in ((0, ahead * over), (1, back * under)):
            hi, lo = split(m)
            G[a, l * rows : (l + 1) * rows] = hi
            G[a, n_rows + l * rows : n_rows + (l + 1) * rows] = lo


def split(x):
    hi = x.astype(jnp.bfloat16)
    return hi, (x - hi.astype(jnp.float32)).astype(jnp.bfloat16)


def kernel(
    dims, ctrl, pert, mask, wgt, classes, lat_tab, lon_tab, lev, out,
    X, Q, Wt, Mk, S, SR, CR, U, Y, D, V, F, R1, R2, WH, B, GS,
    loc, ysend, yrecv, xsend, xrecv, csend, crecv, s1, r1, s2, r2, s3, r3, s4, r4, s5, r5,
):
    n_mem, n_lat, n_lon, members, levels, rows, cols, taps, nt = dims
    h = taps // 2
    nb = cols // LANES + 1
    width = nb * LANES
    rt_n = rows // SUB
    ext = rows + 2 * SUB
    chips = n_mem // 2
    quarter = nt // 4
    shard = quarter // chips
    edge = levels * nb
    n_quarter = levels * rt_n // 4

    def tile_of(idx):
        return idx // n_quarter * quarter + lax.rem(idx, n_quarter) * nb

    mem, lat, lon = lax.axis_index("mem"), lax.axis_index("lat"), lax.axis_index("lon")
    z, c = mem // 2, lax.rem(mem, 2)
    sib = mem + 1 - 2 * c
    lon_to = [lax.rem(lon + 1, n_lon)] + ([lax.rem(lon + n_lon - 1, n_lon)] if n_lon > 2 else [])
    lat_to = ((lat - 1, lat > 0, 1), (lat + 1, lat < n_lat - 1, 0))

    main = pl.ds(SUB, rows)
    loads = [
        pltpu.make_async_copy(ctrl, X.at[:, :, main, pl.ds(0, cols)], loc.at[0]),
        pltpu.make_async_copy(pert, Q.at[:, :, main, pl.ds(0, cols)], loc.at[1]),
        pltpu.make_async_copy(wgt, Wt, loc.at[2]),
        pltpu.make_async_copy(mask, Mk, loc.at[3]),
    ]
    for load in loads:
        load.start()

    barrier = pltpu.get_barrier_semaphore()

    def greet(**where):
        pl.semaphore_signal(barrier, inc=1, device_id=where, device_id_type=pl.DeviceIdType.MESH)

    greet(mem=sib)
    for k in range(1, chips):
        greet(mem=lax.rem(z + k, chips) * 2 + c)
    for x in lon_to:
        greet(lon=x)
    for there, exists, _ in lat_to:
        @pl.when(exists)
        def _():
            greet(lat=there)
            greet(lat=there, mem=sib)
            for x in lon_to:
                greet(lat=there, lon=x)
    matrices(lat, classes, lat_tab, lon_tab, lev, GS, B, levels, rows)
    n_rows = levels * rows

    peers = chips + len(lon_to)
    for _, exists, _ in lat_to:
        peers += jnp.where(exists, 2 + len(lon_to), 0)
    pl.semaphore_wait(barrier, peers)

    def remote(src, dst, send, recv, **where):
        return pltpu.make_async_remote_copy(
            src_ref=src, dst_ref=dst, send_sem=send, recv_sem=recv,
            device_id=where, device_id_type=pl.DeviceIdType.MESH,
        )

    def row_copies(side, there):
        mine = pl.ds(0 if side else rows - SUB, SUB)
        its = pl.ds(rows + SUB if side else 0, SUB)
        return [
            remote(src.at[:, :, mine], dst.at[:, :, its, pl.ds(0, cols)], ysend.at[side, a], yrecv.at[side, a], lat=there)
            for a, (src, dst) in enumerate(((ctrl, X), (pert, Q)))
        ]

    for there, exists, side in lat_to:
        @pl.when(exists)
        def _():
            row_copies(side, there)[0].start()

    lane = lax.broadcasted_iota(jnp.int32, (SUB, LANES), 1)
    windows = [(16, 32 * m) for m in range(members)]
    centre = 32 * members - 8
    windows += [(8, centre + 16 * m) for m in range(members)] + [(8, centre + 16 * members)]
    assert centre + 16 * members + 24 <= LANES

    for load in loads:
        load.wait()

    def pack(idx, carry):
        l, r = idx // rt_n, pl.multiple_of(lax.rem(idx, rt_n) * SUB, SUB)
        total = jnp.zeros((SUB, LANES), jnp.float32)
        here, inner = pl.ds(r, SUB), pl.ds(r + SUB, SUB)
        first, last = pl.ds(0, LANES), pl.ds(cols - LANES, LANES)
        wm = [Wt[l, here, at] * Mk[l, here, at].astype(jnp.float32) for at in (first, last)]
        ends = [(X[m, l, inner, first], X[m, l, inner, last]) for m in range(members)]
        ends += [(Q[m, l, inner, first], Q[m, l, inner, last]) for m in range(members)]
        ends += [tuple(wm)]
        for (reach, at), (low, high) in zip(windows, ends):
            part = jnp.where(lane < reach, low, jnp.where(lane >= LANES - reach, high, 0.0))
            total += pltpu.roll(part, at, 1) if at else part
        S[l, here] = total
        return carry

    lax.fori_loop(0, levels * rt_n, pack, 0)

    strips = [remote(S, SR.at[a], xsend.at[a], xrecv.at[a], lon=x) for a, x in enumerate(lon_to)]
    for copy in strips:
        copy.start()

    def corner_copies(side, there):
        mine = pl.ds(0 if side else rows - SUB, SUB)
        return [
            remote(S.at[:, mine], CR.at[side, a], csend.at[side, a], crecv.at[side, a], lat=there, lon=x)
            for a, x in enumerate(lon_to)
        ]

    for there, exists, side in lat_to:
        @pl.when(exists)
        def _():
            for copy in corner_copies(side, there):
                copy.start()

    for side, there, exists in ((0, lat - 1, lat > 0), (1, lat + 1, lat < n_lat - 1)):
        its = pl.ds(rows + SUB if side else 0, SUB)

        @pl.when(jnp.logical_not(exists))
        def _():
            for m in range(members):
                for l in range(levels):
                    X[m, l, its] = jnp.zeros((SUB, width), jnp.float32)
                    Y[m, l, its] = jnp.zeros((SUB, cols), jnp.float32)

    def weigh(idx, carry):
        rt, l = idx // levels, lax.rem(idx, levels)
        r = pl.ds(pl.multiple_of(rt * SUB, SUB), SUB)
        for b in range(nb - 1):
            at = pl.ds(b * LANES, LANES)
            V[tile_of(idx) + b] = Wt[l, r, at] * Mk[l, r, at].astype(jnp.float32)
        return carry

    lax.fori_loop(0, levels * rt_n, weigh, 0)

    def unpack(w, read):
        at = windows[w][1]
        got = read(0) if n_lon == 2 else None
        if got is None:
            a, b = read(1), read(0)
            a = pltpu.roll(a, LANES - at, 1) if at else a
            b = pltpu.roll(b, LANES - at, 1) if at else b
            return jnp.where(lane < LANES // 2, a, b)
        return pltpu.roll(got, LANES - at, 1) if at else got

    for copy in strips:
        copy.wait()
    strip = pl.ds(cols, LANES)

    def spread_strip(idx, carry):
        rt, l = idx // levels, lax.rem(idx, levels)
        r = pl.multiple_of(rt * SUB, SUB)
        for w in range(2 * members + 1):
            value = unpack(w, lambda a: SR[a, l, pl.ds(r, SUB)])
            if w < members:
                X[w, l, pl.ds(r + SUB, SUB), strip] = value
            elif w < 2 * members:
                Q[w - members, l, pl.ds(r + SUB, SUB), strip] = value
            else:
                V[tile_of(idx) + nb - 1] = value
        return carry

    lax.fori_loop(0, levels * rt_n, spread_strip, 0)

    for there, exists, side in lat_to:
        @pl.when(exists)
        def _():
            row_copies(side, there)[0].wait_send()
            row_copies(side, there)[1].start()
            for copy in corner_copies(side, there):
                copy.wait_send()
    for side, there, exists in ((0, lat - 1, lat > 0), (1, lat + 1, lat < n_lat - 1)):
        its = pl.ds(rows + SUB if side else 0, SUB)

        @pl.when(exists)
        def _():
            row_copies(side, there)[0].wait_recv()
            for copy in corner_copies(side, there):
                copy.wait_recv()
            for l in range(levels):
                for w in range(2 * members):
                    value = unpack(w, lambda a: CR[side, a, l])
                    if w < members:
                        X[w, l, its, strip] = value
                    else:
                        Q[w - members, l, its, strip] = value

    def product(a, x):
        hi, lo = split(x)
        f32 = jnp.float32
        both = jnp.dot(GS[a], hi, preferred_element_type=f32)
        return both[:n_rows] + both[n_rows:] + jnp.dot(GS[a, 0:n_rows], lo, preferred_element_type=f32)

    for m in range(members):
        for lo_col in range(0, width, 2 * LANES):
            w = min(2 * LANES, width - lo_col)
            x = X[m, :, :, lo_col : lo_col + w].reshape(levels * ext, w)
            U[m, :, :, lo_col : lo_col + w] = product(0, x).reshape(levels, rows, w)

    def along(u, tile, forward):
        total = None
        for t in range(taps):
            s = (h - t) if forward else (t - h)
            moved = pltpu.roll(u, s % width, 1) if s else u
            coef = B[t, pl.ds(pl.multiple_of(tile * SUB, SUB), SUB)]
            term = jnp.concatenate([coef] * nb, axis=1) * moved
            total = term if total is None else total + term
        return total

    def forward(idx, carry):
        rt, l = idx // levels, lax.rem(idx, levels)
        r = pl.multiple_of(rt * SUB, SUB)
        total = None
        for m in range(members):
            term = Q[m, l, pl.ds(r + SUB, SUB)] * along(U[m, l, pl.ds(r, SUB)], rt + 1, True)
            total = term if total is None else total + term
        for b in range(nb):
            D[tile_of(idx) + b] = total[:, b * LANES : (b + 1) * LANES]
        return carry

    for g in range(4):
        for i in range(n_quarter * nb, quarter):
            D[g * quarter + i] = jnp.zeros((SUB, LANES), jnp.float32)
            V[g * quarter + i] = jnp.zeros((SUB, LANES), jnp.float32)

    own_q = [step + c * (3 - 2 * step) for step in range(2)]
    sib_q = [step + (1 - c) * (3 - 2 * step) for step in range(2)]

    def over(q, body):
        lax.fori_loop(q * n_quarter, q * n_quarter + n_quarter, body, 0)

    def part(q, chip):
        return pl.ds(q * quarter + chip * shard, shard)

    pairs, to_owner, back, passed = [], [[], []], [[], []], [[], []]
    for step in range(2):
        over(sib_q[step], forward)
        pair = remote(D.at[pl.ds(sib_q[step] * quarter, quarter)], R1.at[step], s1.at[step], r1.at[step], mem=sib)
        pair.start()
        pairs.append(pair)
    for step in range(2):
        over(own_q[step], forward)
        pairs[step].wait_recv()
        for k in range(1, chips):
            tz = lax.rem(z + k, chips)
            here = part(own_q[step], tz)
            D[here] += R1[step, pl.ds(tz * shard, shard)]
            copy = remote(D.at[here], R2.at[step, k - 1], s2.at[step, k - 1], r2.at[step, k - 1], mem=tz * 2 + c)
            copy.start()
            to_owner[step].append(copy)
    for step in range(2):
        for copy in to_owner[step]:
            copy.wait_recv()
        here = part(own_q[step], z)
        total = D[here] + R1[step, pl.ds(z * shard, shard)]
        for k in range(1, chips):
            total += R2[step, k - 1]
        F[here] = total * V[here]
        mine = F.at[here]
        for k in range(1, chips):
            copy = remote(mine, mine, s3.at[step, k - 1], r3.at[step, k - 1], mem=lax.rem(z + k, chips) * 2 + c)
            copy.start()
            back[step].append(copy)
        copy = remote(mine, mine, s4.at[step, 0], r4.at[step, 0], mem=sib)
        copy.start()
        passed[step].append(copy)

    def edge_copies(side, there):
        at = 0 if side else 3 * quarter + n_quarter * nb - edge
        return [
            remote(F.at[pl.ds(at, edge)], WH.at[side], s5.at[side, a], r5.at[side], lat=there, mem=m)
            for a, m in enumerate((mem, sib))
        ]

    def backward_tile(l, r, tile, read):
        w = jnp.concatenate([read(b) for b in range(nb)], axis=1)
        for m in range(members):
            Y[m, l, pl.ds(r, SUB)] = along(Q[m, l, pl.ds(r, SUB)] * w, tile, False)[:, :cols]

    def backward(idx, carry):
        rt, l = idx // levels, lax.rem(idx, levels)
        r = pl.multiple_of(rt * SUB + SUB, SUB)
        backward_tile(l, r, rt + 1, lambda b: F[tile_of(idx) + b])
        return carry

    for step in range(2):
        for k in range(1, chips):
            back[step][k - 1].wait_recv()
            got = F.at[part(own_q[step], lax.rem(z - k + chips, chips))]
            copy = remote(got, got, s4.at[step, k], r4.at[step, k], mem=sib)
            copy.start()
            passed[step].append(copy)
        if step == 0:
            for there, exists, side in lat_to:
                @pl.when(exists & (c == 1 - side))
                def _():
                    for copy in edge_copies(side, there):
                        copy.start()
        over(own_q[step], backward)
    for step in range(2):
        for copy in passed[step]:
            copy.wait_recv()
        over(sib_q[step], backward)

    for side, there, exists in ((0, lat - 1, lat > 0), (1, lat + 1, lat < n_lat - 1)):
        tile = rt_n + 1 if side else 0

        @pl.when(exists)
        def _():
            row_copies(side, there)[1].wait_recv()
            edge_copies(side, there)[0].wait_recv()

            def halo(l, carry):
                backward_tile(l, tile * SUB, tile, lambda b: WH[side, l * nb + b])
                return carry

            lax.fori_loop(0, levels, halo, 0)

    for m in range(members):
        for lo_col in range(0, cols, 2 * LANES):
            at = slice(lo_col, lo_col + 2 * LANES)
            y = Y[m, :, :, at].reshape(levels * ext, 2 * LANES)
            out[m, :, :, at] = X[m, :, SUB : SUB + rows, at] + product(1, y).reshape(levels, rows, 2 * LANES)

    for copy in pairs + to_owner[0] + to_owner[1] + back[0] + back[1] + passed[0] + passed[1]:
        copy.wait_send()
    for there, exists, side in lat_to:
        @pl.when(exists)
        def _():
            row_copies(side, there)[1].wait_send()

        @pl.when(exists & (c == 1 - side))
        def _():
            for copy in edge_copies(side, there):
                copy.wait_send()


def solution(mesh):
    n_mem, n_lat, n_lon = mesh.shape["mem"], mesh.shape["lat"], mesh.shape["lon"]

    def per_device(controls, perturbations, obs_mask, obs_weight, lat_class, lat_table, lon_table, lev_table):
        members, levels, rows, cols = controls.shape
        taps = lat_table.shape[1]
        nb = cols // LANES + 1
        width, ext, rt_n = nb * LANES, rows + 2 * SUB, rows // SUB
        nt = 4 * (-(-(levels * rt_n // 4 * nb) // (n_mem // 2)) * (n_mem // 2))
        chips = n_mem // 2
        shard = nt // 4 // chips
        dims = (n_mem, n_lat, n_lon, members, levels, rows, cols, taps, nt)
        f32 = jnp.float32
        dma = pltpu.SemaphoreType.DMA
        sides = 1 if n_lon == 2 else 2
        hbm, vmem = pl.BlockSpec(memory_space=pl.ANY), pl.BlockSpec(memory_space=pltpu.VMEM)
        tiles = lambda *n: pltpu.VMEM((*n, SUB, LANES), f32)
        return pl.pallas_call(
            functools.partial(kernel, dims),
            out_shape=jax.ShapeDtypeStruct(controls.shape, f32),
            in_specs=[hbm] * 4 + [vmem] * 3 + [pl.BlockSpec(memory_space=pltpu.SMEM)],
            out_specs=vmem,
            scratch_shapes=[
                pltpu.VMEM((members, levels, ext, width), f32),
                pltpu.VMEM((members, levels, ext, width), f32),
                pltpu.VMEM((levels, rows, cols), f32),
                pltpu.VMEM((levels, rows, cols), jnp.int32),
                pltpu.VMEM((levels, rows, LANES), f32),
                pltpu.VMEM((sides, levels, rows, LANES), f32),
                pltpu.VMEM((2, sides, levels, SUB, LANES), f32),
                pltpu.VMEM((members, levels, rows, width), f32),
                pltpu.VMEM((members, levels, ext, cols), f32),
                tiles(nt), tiles(nt), tiles(nt),
                tiles(2, nt // 4), tiles(2, max(chips - 1, 1), shard), tiles(2, levels * nb),
                pltpu.VMEM((taps, ext, LANES), f32),
                pltpu.VMEM((2, 2 * levels * rows, levels * ext), jnp.bfloat16),
                dma((4,)), dma((2, 2)), dma((2, 2)), dma((sides,)), dma((sides,)), dma((2, sides)), dma((2, sides)),
                dma((2,)), dma((2,)), *[dma((2, chips))] * 6, dma((2, 2)), dma((2,)),
            ],
            compiler_params=pltpu.CompilerParams(
                collective_id=0, has_side_effects=True, vmem_limit_bytes=62 * 1024 * 1024
            ),
        )(controls, perturbations, obs_mask, obs_weight, lat_class[None], lat_table, lon_table, lev_table)

    return jax.shard_map(
        per_device,
        mesh=mesh,
        in_specs=(
            P("mem", None, "lat", "lon"),
            P("mem", None, "lat", "lon"),
            P(None, "lat", "lon"),
            P(None, "lat", "lon"),
            P(),
            P(),
            P(),
            P(),
        ),
        out_specs=P("mem", None, "lat", "lon"),
        check_vma=False,
    )
```

```python
import functools

import jax
import jax.numpy as jnp
from jax import lax
from jax.experimental import pallas as pl
from jax.experimental.pallas import tpu as pltpu
from jax.sharding import PartitionSpec as P

LANES = 128
SUB = 8


PRECISE = lax.Precision.HIGHEST


def contract(a, b, precision=None):
    return lax.dot_general(
        a, b, (((0,), (0,)), ((), ())), precision=precision, preferred_element_type=jnp.float32
    )


def matrices(lat, classes, lat_tab, lon_tab, lev, G, B, levels, rows):
    n_classes, taps = lat_tab.shape
    n_lat = classes.shape[1]
    h = taps // 2
    ext = rows + 2 * SUB
    wide, n_rows = levels * ext, levels * rows
    start = lat * rows - SUB
    hit = lax.broadcasted_iota(jnp.int32, (n_classes, n_lat), 0) == classes[...]
    block = lax.broadcasted_iota(jnp.int32, (1, wide), 1)
    for l in range(1, levels):
        block = jnp.where(lax.broadcasted_iota(jnp.int32, (1, wide), 1) >= l * ext, block - ext, block)
    level = lax.broadcasted_iota(jnp.int32, (1, wide), 1)
    pick = lax.broadcasted_iota(jnp.int32, (n_lat, wide), 0) == block + start
    one = lambda x: jnp.where(x, 1.0, 0.0)
    onehot = jnp.dot(one(hit), one(pick), preferred_element_type=jnp.float32)
    onehot_ext = onehot[:, :ext]
    lat_rows = contract(onehot_ext, lat_tab[...], PRECISE)
    lat_lanes = contract(lat_tab[...], onehot, PRECISE)
    lon_rows = contract(onehot_ext, lon_tab[...], PRECISE)
    for t in range(taps):
        B[t] = jnp.broadcast_to(lon_rows[:, t : t + 1], (ext, LANES))
    i = lax.broadcasted_iota(jnp.int32, (rows, wide), 0)
    e = block - SUB
    inside = (e + lat * rows >= 0) & (e + lat * rows < n_lat)
    ahead = jnp.zeros((rows, wide), jnp.float32)
    back = jnp.zeros((rows, wide), jnp.float32)
    for t in range(taps):
        ahead = jnp.where((e - i + h == t) & inside, lat_rows[SUB : SUB + rows, t : t + 1], ahead)
        back = jnp.where(i - e + h == t, lat_lanes[t : t + 1, :], back)
    for l in range(levels):
        over, under = jnp.zeros((1, wide), jnp.float32), jnp.zeros((1, wide), jnp.float32)
        for p in range(levels):
            there = (level >= p * ext) & (level < (p + 1) * ext)
            if abs(p - l) <= h:
                over = jnp.where(there, lev[l, p - l + h], over)
                under = jnp.where(there, lev[p, l - p + h], under)
        for a, m in ((0, ahead * over), (1, back * under)):
            hi, lo = split(m)
            G[a, l * rows : (l + 1) * rows] = hi
            G[a, n_rows + l * rows : n_rows + (l + 1) * rows] = lo


def split(x):
    hi = x.astype(jnp.bfloat16)
    return hi, (x - hi.astype(jnp.float32)).astype(jnp.bfloat16)


def kernel(
    dims, ctrl, pert, mask, wgt, classes, lat_tab, lon_tab, lev, out,
    X, Q, Wt, Mk, S, SR, CR, U, Y, D, V, F, R1, R2, WH, B, GS,
    loc, ysend, yrecv, xsend, xrecv, csend, crecv, s1, r1, s2, r2, s3, r3, s4, r4, s5, r5,
):
    n_mem, n_lat, n_lon, members, levels, rows, cols, taps, nt = dims
    h = taps // 2
    nb = cols // LANES + 1
    width = nb * LANES
    rt_n = rows // SUB
    ext = rows + 2 * SUB
    chips = n_mem // 2
    quarter = nt // 4
    shard = quarter // chips
    edge = levels * nb
    n_quarter = levels * rt_n // 4

    def tile_of(idx):
        return idx // n_quarter * quarter + lax.rem(idx, n_quarter) * nb

    mem, lat, lon = lax.axis_index("mem"), lax.axis_index("lat"), lax.axis_index("lon")
    z, c = mem // 2, lax.rem(mem, 2)
    sib = mem + 1 - 2 * c
    lon_to = [lax.rem(lon + 1, n_lon)] + ([lax.rem(lon + n_lon - 1, n_lon)] if n_lon > 2 else [])
    lat_to = ((lat - 1, lat > 0, 1), (lat + 1, lat < n_lat - 1, 0))

    main = pl.ds(SUB, rows)
    loads = [
        pltpu.make_async_copy(ctrl, X.at[:, :, main, pl.ds(0, cols)], loc.at[0]),
        pltpu.make_async_copy(pert, Q.at[:, :, main, pl.ds(0, cols)], loc.at[1]),
        pltpu.make_async_copy(wgt, Wt, loc.at[2]),
        pltpu.make_async_copy(mask, Mk, loc.at[3]),
    ]
    for load in loads:
        load.start()

    barrier = pltpu.get_barrier_semaphore()

    def greet(**where):
        pl.semaphore_signal(barrier, inc=1, device_id=where, device_id_type=pl.DeviceIdType.MESH)

    greet(mem=sib)
    for k in range(1, chips):
        greet(mem=lax.rem(z + k, chips) * 2 + c)
    for x in lon_to:
        greet(lon=x)
    for there, exists, _ in lat_to:
        @pl.when(exists)
        def _():
            greet(lat=there)
            greet(lat=there, mem=sib)
            for x in lon_to:
                greet(lat=there, lon=x)
    matrices(lat, classes, lat_tab, lon_tab, lev, GS, B, levels, rows)
    n_rows = levels * rows

    lane = lax.broadcasted_iota(jnp.int32, (SUB, LANES), 1)
    windows = [(16, 32 * m) for m in range(members)]
    centre = 32 * members - 8
    windows += [(8, centre + 16 * m) for m in range(members)] + [(8, centre + 16 * members)]
    assert centre + 16 * members + 24 <= LANES

    for load in loads:
        load.wait()

    def pack(idx, carry):
        l, r = idx // rt_n, pl.multiple_of(lax.rem(idx, rt_n) * SUB, SUB)
        total = jnp.zeros((SUB, LANES), jnp.float32)
        here, inner = pl.ds(r, SUB), pl.ds(r + SUB, SUB)
        first, last = pl.ds(0, LANES), pl.ds(cols - LANES, LANES)
        wm = [Wt[l, here, at] * Mk[l, here, at].astype(jnp.float32) for at in (first, last)]
        ends = [(X[m, l, inner, first], X[m, l, inner, last]) for m in range(members)]
        ends += [(Q[m, l, inner, first], Q[m, l, inner, last]) for m in range(members)]
        ends += [tuple(wm)]
        for (reach, at), (low, high) in zip(windows, ends):
            part = jnp.where(lane < reach, low, jnp.where(lane >= LANES - reach, high, 0.0))
            total += pltpu.roll(part, at, 1) if at else part
        S[l, here] = total
        return carry

    lax.fori_loop(0, levels * rt_n, pack, 0)

    peers = chips + len(lon_to)
    for _, exists, _ in lat_to:
        peers += jnp.where(exists, 2 + len(lon_to), 0)
    pl.semaphore_wait(barrier, peers)

    def remote(src, dst, send, recv, **where):
        return pltpu.make_async_remote_copy(
            src_ref=src, dst_ref=dst, send_sem=send, recv_sem=recv,
            device_id=where, device_id_type=pl.DeviceIdType.MESH,
        )

    def row_copies(side, there):
        mine = pl.ds(0 if side else rows - SUB, SUB)
        its = pl.ds(rows + SUB if side else 0, SUB)
        return [
            remote(src.at[:, :, mine], dst.at[:, :, its, pl.ds(0, cols)], ysend.at[side, a], yrecv.at[side, a], lat=there)
            for a, (src, dst) in enumerate(((ctrl, X), (pert, Q)))
        ]

    for there, exists, side in lat_to:
        @pl.when(exists)
        def _():
            row_copies(side, there)[0].start()

    strips = [remote(S, SR.at[a], xsend.at[a], xrecv.at[a], lon=x) for a, x in enumerate(lon_to)]
    for copy in strips:
        copy.start()

    def corner_copies(side, there):
        mine = pl.ds(0 if side else rows - SUB, SUB)
        return [
            remote(S.at[:, mine], CR.at[side, a], csend.at[side, a], crecv.at[side, a], lat=there, lon=x)
            for a, x in enumerate(lon_to)
        ]

    for there, exists, side in lat_to:
        @pl.when(exists)
        def _():
            for copy in corner_copies(side, there):
                copy.start()

    for side, there, exists in ((0, lat - 1, lat > 0), (1, lat + 1, lat < n_lat - 1)):
        its = pl.ds(rows + SUB if side else 0, SUB)

        @pl.when(jnp.logical_not(exists))
        def _():
            for m in range(members):
                for l in range(levels):
                    X[m, l, its] = jnp.zeros((SUB, width), jnp.float32)
                    Y[m, l, its] = jnp.zeros((SUB, cols), jnp.float32)

    def weigh(idx, carry):
        rt, l = idx // levels, lax.rem(idx, levels)
        r = pl.ds(pl.multiple_of(rt * SUB, SUB), SUB)
        for b in range(nb - 1):
            at = pl.ds(b * LANES, LANES)
            V[tile_of(idx) + b] = Wt[l, r, at] * Mk[l, r, at].astype(jnp.float32)
        return carry

    lax.fori_loop(0, levels * rt_n, weigh, 0)

    def unpack(w, read):
        at = windows[w][1]
        got = read(0) if n_lon == 2 else None
        if got is None:
            a, b = read(1), read(0)
            a = pltpu.roll(a, LANES - at, 1) if at else a
            b = pltpu.roll(b, LANES - at, 1) if at else b
            return jnp.where(lane < LANES // 2, a, b)
        return pltpu.roll(got, LANES - at, 1) if at else got

    for copy in strips:
        copy.wait()
    strip = pl.ds(cols, LANES)

    def spread_strip(idx, carry):
        rt, l = idx // levels, lax.rem(idx, levels)
        r = pl.multiple_of(rt * SUB, SUB)
        for w in range(2 * members + 1):
            value = unpack(w, lambda a: SR[a, l, pl.ds(r, SUB)])
            if w < members:
                X[w, l, pl.ds(r + SUB, SUB), strip] = value
            elif w < 2 * members:
                Q[w - members, l, pl.ds(r + SUB, SUB), strip] = value
            else:
                V[tile_of(idx) + nb - 1] = value
        return carry

    lax.fori_loop(0, levels * rt_n, spread_strip, 0)

    for there, exists, side in lat_to:
        @pl.when(exists)
        def _():
            row_copies(side, there)[0].wait_send()
            row_copies(side, there)[1].start()
            for copy in corner_copies(side, there):
                copy.wait_send()
    for side, there, exists in ((0, lat - 1, lat > 0), (1, lat + 1, lat < n_lat - 1)):
        its = pl.ds(rows + SUB if side else 0, SUB)

        @pl.when(exists)
        def _():
            row_copies(side, there)[0].wait_recv()
            for copy in corner_copies(side, there):
                copy.wait_recv()
            for l in range(levels):
                for w in range(2 * members):
                    value = unpack(w, lambda a: CR[side, a, l])
                    if w < members:
                        X[w, l, its, strip] = value
                    else:
                        Q[w - members, l, its, strip] = value

    def product(a, x):
        hi, lo = split(x)
        f32 = jnp.float32
        both = jnp.dot(GS[a], hi, preferred_element_type=f32)
        return both[:n_rows] + both[n_rows:] + jnp.dot(GS[a, 0:n_rows], lo, preferred_element_type=f32)

    for m in range(members):
        for lo_col in range(0, width, 2 * LANES):
            w = min(2 * LANES, width - lo_col)
            x = X[m, :, :, lo_col : lo_col + w].reshape(levels * ext, w)
            U[m, :, :, lo_col : lo_col + w] = product(0, x).reshape(levels, rows, w)

    def along(u, tile, forward):
        total = None
        for t in range(taps):
            s = (h - t) if forward else (t - h)
            moved = pltpu.roll(u, s % width, 1) if s else u
            coef = B[t, pl.ds(pl.multiple_of(tile * SUB, SUB), SUB)]
            term = jnp.concatenate([coef] * nb, axis=1) * moved
            total = term if total is None else total + term
        return total

    def forward(idx, carry):
        rt, l = idx // levels, lax.rem(idx, levels)
        r = pl.multiple_of(rt * SUB, SUB)
        total = None
        for m in range(members):
            term = Q[m, l, pl.ds(r + SUB, SUB)] * along(U[m, l, pl.ds(r, SUB)], rt + 1, True)
            total = term if total is None else total + term
        for b in range(nb):
            D[tile_of(idx) + b] = total[:, b * LANES : (b + 1) * LANES]
        return carry

    for g in range(4):
        for i in range(n_quarter * nb, quarter):
            D[g * quarter + i] = jnp.zeros((SUB, LANES), jnp.float32)
            V[g * quarter + i] = jnp.zeros((SUB, LANES), jnp.float32)

    own_q = [step + c * (3 - 2 * step) for step in range(2)]
    sib_q = [step + (1 - c) * (3 - 2 * step) for step in range(2)]

    def over(q, body):
        lax.fori_loop(q * n_quarter, q * n_quarter + n_quarter, body, 0)

    def part(q, chip):
        return pl.ds(q * quarter + chip * shard, shard)

    pairs, to_owner, back, passed = [], [[], []], [[], []], [[], []]
    for step in range(2):
        over(sib_q[step], forward)
        pair = remote(D.at[pl.ds(sib_q[step] * quarter, quarter)], R1.at[step], s1.at[step], r1.at[step], mem=sib)
        pair.start()
        pairs.append(pair)
    for step in range(2):
        over(own_q[step], forward)
        pairs[step].wait_recv()
        for k in range(1, chips):
            tz = lax.rem(z + k, chips)
            here = part(own_q[step], tz)
            D[here] += R1[step, pl.ds(tz * shard, shard)]
            copy = remote(D.at[here], R2.at[step, k - 1], s2.at[step, k - 1], r2.at[step, k - 1], mem=tz * 2 + c)
            copy.start()
            to_owner[step].append(copy)
    for step in range(2):
        for copy in to_owner[step]:
            copy.wait_recv()
        here = part(own_q[step], z)
        total = D[here] + R1[step, pl.ds(z * shard, shard)]
        for k in range(1, chips):
            total += R2[step, k - 1]
        F[here] = total * V[here]
        mine = F.at[here]
        for k in range(1, chips):
            copy = remote(mine, mine, s3.at[step, k - 1], r3.at[step, k - 1], mem=lax.rem(z + k, chips) * 2 + c)
            copy.start()
            back[step].append(copy)
        copy = remote(mine, mine, s4.at[step, 0], r4.at[step, 0], mem=sib)
        copy.start()
        passed[step].append(copy)

    def edge_copies(side, there):
        at = 0 if side else 3 * quarter + n_quarter * nb - edge
        return [
            remote(F.at[pl.ds(at, edge)], WH.at[side], s5.at[side, a], r5.at[side], lat=there, mem=m)
            for a, m in enumerate((mem, sib))
        ]

    def backward_tile(l, r, tile, read):
        w = jnp.concatenate([read(b) for b in range(nb)], axis=1)
        for m in range(members):
            Y[m, l, pl.ds(r, SUB)] = along(Q[m, l, pl.ds(r, SUB)] * w, tile, False)[:, :cols]

    def backward(idx, carry):
        rt, l = idx // levels, lax.rem(idx, levels)
        r = pl.multiple_of(rt * SUB + SUB, SUB)
        backward_tile(l, r, rt + 1, lambda b: F[tile_of(idx) + b])
        return carry

    for step in range(2):
        for k in range(1, chips):
            back[step][k - 1].wait_recv()
            got = F.at[part(own_q[step], lax.rem(z - k + chips, chips))]
            copy = remote(got, got, s4.at[step, k], r4.at[step, k], mem=sib)
            copy.start()
            passed[step].append(copy)
        if step == 0:
            for there, exists, side in lat_to:
                @pl.when(exists & (c == 1 - side))
                def _():
                    for copy in edge_copies(side, there):
                        copy.start()
        over(own_q[step], backward)
    for step in range(2):
        for copy in passed[step]:
            copy.wait_recv()
        over(sib_q[step], backward)

    for side, there, exists in ((0, lat - 1, lat > 0), (1, lat + 1, lat < n_lat - 1)):
        tile = rt_n + 1 if side else 0

        @pl.when(exists)
        def _():
            row_copies(side, there)[1].wait_recv()
            edge_copies(side, there)[0].wait_recv()

            def halo(l, carry):
                backward_tile(l, tile * SUB, tile, lambda b: WH[side, l * nb + b])
                return carry

            lax.fori_loop(0, levels, halo, 0)

    for m in range(members):
        for lo_col in range(0, cols, 2 * LANES):
            at = slice(lo_col, lo_col + 2 * LANES)
            y = Y[m, :, :, at].reshape(levels * ext, 2 * LANES)
            out[m, :, :, at] = X[m, :, SUB : SUB + rows, at] + product(1, y).reshape(levels, rows, 2 * LANES)

    for copy in pairs + to_owner[0] + to_owner[1] + back[0] + back[1] + passed[0] + passed[1]:
        copy.wait_send()
    for there, exists, side in lat_to:
        @pl.when(exists)
        def _():
            row_copies(side, there)[1].wait_send()

        @pl.when(exists & (c == 1 - side))
        def _():
            for copy in edge_copies(side, there):
                copy.wait_send()


def solution(mesh):
    n_mem, n_lat, n_lon = mesh.shape["mem"], mesh.shape["lat"], mesh.shape["lon"]

    def per_device(controls, perturbations, obs_mask, obs_weight, lat_class, lat_table, lon_table, lev_table):
        members, levels, rows, cols = controls.shape
        taps = lat_table.shape[1]
        nb = cols // LANES + 1
        width, ext, rt_n = nb * LANES, rows + 2 * SUB, rows // SUB
        nt = 4 * (-(-(levels * rt_n // 4 * nb) // (n_mem // 2)) * (n_mem // 2))
        chips = n_mem // 2
        shard = nt // 4 // chips
        dims = (n_mem, n_lat, n_lon, members, levels, rows, cols, taps, nt)
        f32 = jnp.float32
        dma = pltpu.SemaphoreType.DMA
        sides = 1 if n_lon == 2 else 2
        hbm, vmem = pl.BlockSpec(memory_space=pl.ANY), pl.BlockSpec(memory_space=pltpu.VMEM)
        tiles = lambda *n: pltpu.VMEM((*n, SUB, LANES), f32)
        return pl.pallas_call(
            functools.partial(kernel, dims),
            out_shape=jax.ShapeDtypeStruct(controls.shape, f32),
            in_specs=[hbm] * 4 + [vmem] * 3 + [pl.BlockSpec(memory_space=pltpu.SMEM)],
            out_specs=vmem,
            scratch_shapes=[
                pltpu.VMEM((members, levels, ext, width), f32),
                pltpu.VMEM((members, levels, ext, width), f32),
                pltpu.VMEM((levels, rows, cols), f32),
                pltpu.VMEM((levels, rows, cols), jnp.int32),
                pltpu.VMEM((levels, rows, LANES), f32),
                pltpu.VMEM((sides, levels, rows, LANES), f32),
                pltpu.VMEM((2, sides, levels, SUB, LANES), f32),
                pltpu.VMEM((members, levels, rows, width), f32),
                pltpu.VMEM((members, levels, ext, cols), f32),
                tiles(nt), tiles(nt), tiles(nt),
                tiles(2, nt // 4), tiles(2, max(chips - 1, 1), shard), tiles(2, levels * nb),
                pltpu.VMEM((taps, ext, LANES), f32),
                pltpu.VMEM((2, 2 * levels * rows, levels * ext), jnp.bfloat16),
                dma((4,)), dma((2, 2)), dma((2, 2)), dma((sides,)), dma((sides,)), dma((2, sides)), dma((2, sides)),
                dma((2,)), dma((2,)), *[dma((2, chips))] * 6, dma((2, 2)), dma((2,)),
            ],
            compiler_params=pltpu.CompilerParams(
                collective_id=0, has_side_effects=True, vmem_limit_bytes=62 * 1024 * 1024
            ),
        )(controls, perturbations, obs_mask, obs_weight, lat_class[None], lat_table, lon_table, lev_table)

    return jax.shard_map(
        per_device,
        mesh=mesh,
        in_specs=(
            P("mem", None, "lat", "lon"),
            P("mem", None, "lat", "lon"),
            P(None, "lat", "lon"),
            P(None, "lat", "lon"),
            P(),
            P(),
            P(),
            P(),
        ),
        out_specs=P("mem", None, "lat", "lon"),
        check_vma=False,
    )
```
